32 devices in a mesh: ctx: 16 (over z, y, core), head: 2 (over x).
Axes of the slice: x: 2, y: 2, z: 4, core: 2. Of those that a mesh axis runs over, the one named last changes fastest.
Arguments:
- queries: bfloat16 [4096, 8192], P(('ctx', 'head')), may hold values from -200 to 200
- key_rows: bfloat16 [4096, 1024], P(('ctx', 'head')), may hold values from -6 to 6
- value_rows: bfloat16 [4096, 1024], P(('ctx', 'head')), may hold values from -6 to 6
- span_order: int32 [32], replicated, may hold values from 0 to 31, each once
Outputs:
- attended: bfloat16 [4096, 8192], P(('ctx', 'head'))
The draws below stay inside these ranges and needn't reach their ends.
Inputs may be any that keep to these rules, and one draw needn't show every extreme that they name: Stored span j holds sequence positions span_order[j] * 128 to span_order[j] * 128 + 127; each number appears once.
All inputs are finite; a program needn't handle non-finite values.
Results may differ from the reference program's by a relative error of at most 0.005.
Values may be sent and summed in bfloat16 or wider, within the bound.
No kernel may reach another device: no remote copies, remote signals or barrier semaphores. Data moves between devices by JAX's collectives and lax.ppermute only.
A program may use at most 256 MiB of HBM per device.

```python
import math
import jax
import jax.numpy as jnp
from jax import lax

HQ = 64
KVH = 8
HD = 128
SPAN = 128
SEQ = 4096
N_CTX = 16


def paired_draw(key):
    base = jax.random.fold_in(key, 4242)
    first_key, second_key = jax.random.split(base, 2)
    queries = jnp.clip(jax.random.normal(first_key, (SEQ, HQ * HD), jnp.float32), -6.0, 6.0)
    keyset = jnp.clip(jax.random.normal(second_key, (SEQ, KVH * HD), jnp.float32), -6.0, 6.0)
    return (queries, keyset)


def draw_queries(key, part):
    return paired_draw(key)[0].astype(jnp.bfloat16)


def draw_key_rows(key, part):
    return paired_draw(key)[1].astype(jnp.bfloat16)


def steps_of(rng, extent, cuts, smallest, top_value):
    factor_of, own = 1.0, jax.random.fold_in(rng, 6)
    for dim, shards_of in cuts:
        heights = jnp.exp(jax.random.uniform(jax.random.fold_in(own, dim), (shards_of,), jnp.float32, smallest / len(cuts), top_value / len(cuts)))
        factor_of = factor_of * jnp.repeat(heights, extent[dim] // shards_of).reshape([-1 if axis == dim else 1 for axis in range(len(extent))])
    return factor_of


def centred(rng, extent, width, most, pieces=(), kind=jnp.bfloat16):
    level = steps_of(rng, extent, pieces, -0.22, 0.18) if pieces else 1.0
    entries = jax.random.normal(rng, extent, jnp.float32) * width * level
    return jnp.minimum(jnp.maximum(entries, -most), most).astype(kind)


def setup_inputs(seed: int = 0) -> dict:
    seeds = jax.random.split(jax.random.key(seed), 5)
    queries = draw_queries(jax.random.fold_in(seeds[4], 71), 0)
    key_rows = draw_key_rows(jax.random.fold_in(seeds[4], 71), 0)
    value_rows = centred(seeds[2], (SEQ, KVH * HD), 1.0, 6.0, ((0, 32),))
    span_order = jax.random.permutation(seeds[3], 2 * N_CTX).astype(jnp.int32)
    return {"queries": queries, "key_rows": key_rows, "value_rows": value_rows, "span_order": span_order}


def reference(queries, key_rows, value_rows, span_order):
    group_size = HQ // KVH
    scaling = HD ** -0.5
    indices = jnp.arange(SEQ, dtype=jnp.int32)
    positions = (span_order[indices // SPAN] * SPAN + indices % SPAN).astype(jnp.int32)
    block_rows = math.gcd(SEQ, 256)
    block_count = SEQ // block_rows
    query_all = queries.reshape(block_count, block_rows, KVH, group_size, HD)
    key_all = key_rows.reshape(SEQ, KVH, HD)
    value_all = value_rows.reshape(SEQ, KVH, HD)
    query_pos = positions.reshape(block_count, block_rows)

    def one_head(head_index):
        key_head = lax.dynamic_index_in_dim(key_all, head_index, 1, False).astype(jnp.float32)
        value_head = lax.dynamic_index_in_dim(value_all, head_index, 1, False).astype(jnp.float32)
        query_head = lax.dynamic_index_in_dim(query_all, head_index, 2, False)

        def one_block(operands):
            query_block, block_pos = operands
            scores = jnp.einsum("qgd,kd->qgk", query_block.astype(jnp.float32), key_head) * scaling
            visible = positions[None, None, :] <= block_pos[:, None, None]
            scores = jnp.where(visible, scores, -1e30)
            ceiling = jnp.max(scores, axis=-1, keepdims=True)
            weights = jnp.where(visible, jnp.exp(scores - ceiling), 0.0)
            totals = jnp.sum(weights, axis=-1)
            rounded = lax.optimization_barrier(weights.astype(jnp.bfloat16))
            blended = jnp.einsum("qgk,kd->qgd", rounded.astype(jnp.float32), value_head)
            return (blended / totals[..., None]).astype(jnp.bfloat16)

        return lax.map(one_block, (query_head, query_pos))

    outputs = lax.map(one_head, jnp.arange(KVH, dtype=jnp.int32))
    return jnp.transpose(outputs, (1, 2, 0, 3, 4)).reshape(SEQ, HQ * HD)
```

```python
import functools
import math

import jax
import jax.numpy as jnp
from jax import lax
from jax.experimental import pallas as pl
from jax.experimental.pallas import tpu as pltpu
from jax.sharding import Mesh
from jax.sharding import PartitionSpec as P

HQ = 64
KVH = 8
HD = 128
SPAN = 128
GROUP = HQ // KVH
ROWS = GROUP * SPAN
SCALE = HD**-0.5 * math.log2(math.e)
EXTRA = 16
BLOCK = 4
NT = (((1,), (1,)), ((), ()))
GROUP_AXES = ("inner", "head")


def attention_kernel(base, *refs):
    n_kv = len(base)
    where_ref, order_ref, q_ref = refs[:3]
    kv_refs = refs[3 : 3 + n_kv]
    o_ref, k_ref, vt_ref, inv_ref, m_ref, acc_ref = refs[3 + n_kv :]
    step = pl.program_id(0)
    spans = k_ref.shape[0]

    @pl.when(step == 0)
    def _():
        def invert(j, carry):
            inv_ref[order_ref[j]] = j
            return carry

        lax.fori_loop(0, spans, invert, 0)
        for index, kv_ref in enumerate(kv_refs):

            @pl.when(where_ref[1 + index] >= 0)
            def _(kv_ref=kv_ref, index=index):
                for j in range(kv_ref.shape[0]):
                    slot = where_ref[1 + index] + j
                    k_ref[slot] = kv_ref[j, :, :HD]
                    vt_ref[slot, :HD] = kv_ref[j, :, HD:].T
                    vt_ref[slot, HD:] = jnp.ones((EXTRA, SPAN), jnp.bfloat16)

    p = order_ref[where_ref[0] + step]

    def queries():
        return jnp.concatenate([q_ref[:, g * HD : (g + 1) * HD] for g in range(GROUP)], 0)

    def keys_values(first, count):
        slots = [inv_ref[first + t] for t in range(count)]
        return (
            jnp.concatenate([k_ref[s] for s in slots], 0),
            jnp.concatenate([vt_ref[s] for s in slots], 1),
        )

    def scores(keys):
        return lax.dot_general(keys, queries(), NT, preferred_element_type=jnp.float32) * SCALE

    def blend(values, weights):
        return jnp.dot(values, weights.astype(jnp.bfloat16), preferred_element_type=jnp.float32)

    def causal(s):
        key = lax.broadcasted_iota(jnp.int32, (SPAN, ROWS), 0)
        row = lax.broadcasted_iota(jnp.int32, (SPAN, ROWS), 1) % SPAN
        return jnp.where(key <= row, s, -1e30)

    def first_block(count):
        keys, values = keys_values(p + 1 - count, count)
        s = scores(keys)
        own = causal(s[(count - 1) * SPAN :])
        s = jnp.concatenate([s[: (count - 1) * SPAN], own], 0) if count > 1 else own
        m = jnp.max(s, axis=0, keepdims=True)
        m_ref[...] = jnp.broadcast_to(m, m_ref.shape)
        acc_ref[...] = blend(values, jnp.exp2(s - m))

    for count in range(1, BLOCK + 1):

        @pl.when(p % BLOCK == count - 1)
        def _(count=count):
            first_block(count)

    def block(b, carry):
        keys, values = keys_values(b * BLOCK, BLOCK)
        acc_ref[...] += blend(values, jnp.exp2(scores(keys) - m_ref[:1]))
        return carry

    lax.fori_loop(0, p // BLOCK, block, 0)

    @pl.when(jnp.logical_not(jnp.max(acc_ref[HD : HD + 8]) < 1e30))
    def _():
        m_ref[...] = jnp.full_like(m_ref, -1e30)
        acc_ref[...] = jnp.zeros_like(acc_ref)

        def careful(j, carry):
            keys, values = keys_values(j, 1)
            s = scores(keys)
            s = jnp.where(j < p, s, causal(s))
            m_old = m_ref[...]
            m_new = jnp.maximum(m_old, jnp.max(s, axis=0, keepdims=True))
            m_ref[...] = m_new
            acc_ref[...] = acc_ref[...] * jnp.exp2(m_old - m_new)[:1] + blend(values, jnp.exp2(s - m_new[:1]))
            return carry

        lax.fori_loop(0, p + 1, careful, 0)

    result = acc_ref[:HD] / acc_ref[HD : HD + 1]
    for g in range(GROUP):
        o_ref[:, g * HD : (g + 1) * HD] = result[:, g * SPAN : (g + 1) * SPAN].T.astype(o_ref.dtype)


def attention(q, pieces, bases, first_span, span_order):
    q_spans = q.shape[0] // SPAN
    spans = span_order.shape[0]
    where = jnp.stack([first_span, *bases]).astype(jnp.int32)
    grid_spec = pltpu.PrefetchScalarGridSpec(
        num_scalar_prefetch=2,
        grid=(q_spans,),
        in_specs=[pl.BlockSpec((SPAN, GROUP * HD), lambda i, *_: (i, 0))]
        + [pl.BlockSpec(piece.shape, lambda i, *_: (0, 0, 0)) for piece in pieces],
        out_specs=pl.BlockSpec((SPAN, GROUP * HD), lambda i, *_: (i, 0)),
        scratch_shapes=[
            pltpu.VMEM((spans, SPAN, HD), jnp.bfloat16),
            pltpu.VMEM((spans, HD + EXTRA, SPAN), jnp.bfloat16),
            pltpu.SMEM((spans,), jnp.int32),
            pltpu.VMEM((8, ROWS), jnp.float32),
            pltpu.VMEM((HD + EXTRA, ROWS), jnp.float32),
        ],
    )
    elements = q.shape[0] * GROUP * spans * SPAN // 2
    return pl.pallas_call(
        functools.partial(attention_kernel, (0,) * len(pieces)),
        grid_spec=grid_spec,
        out_shape=jax.ShapeDtypeStruct(q.shape, q.dtype),
        compiler_params=pltpu.CompilerParams(vmem_limit_bytes=40 * 2**20),
        cost_estimate=pl.CostEstimate(
            flops=4 * HD * elements, bytes_accessed=4 * q.size + 4 * spans * SPAN * HD, transcendentals=elements
        ),
    )(where, span_order, q, *pieces)


def shards(outer, queries, key_rows, value_rows, span_order):
    rows = queries.shape[0]
    place = lax.axis_index("outer")
    packed = jnp.concatenate([key_rows.reshape(rows, KVH, HD), value_rows.reshape(rows, KVH, HD)], 2)
    own = lax.all_to_all(packed.transpose(1, 0, 2), GROUP_AXES, split_axis=0, concat_axis=0, tiled=False)
    group_rows = KVH * rows
    group_spans = group_rows // SPAN
    own = own.reshape(group_spans, SPAN, 2 * HD)
    q = queries.reshape(rows, KVH, GROUP * HD).transpose(1, 0, 2)
    q = lax.all_to_all(q, GROUP_AXES, split_axis=0, concat_axis=0, tiled=False).reshape(group_rows, GROUP * HD)
    if outer == 4:
        up = lax.ppermute(own, "outer", [(i, (i + 1) % outer) for i in range(outer)])
        down = lax.ppermute(own, "outer", [(i, (i - 1) % outer) for i in range(outer)])
        far_up = lax.ppermute(up, "outer", [(1, 2), (2, 3)])
        far_down = lax.ppermute(down, "outer", [(1, 0), (2, 1)])
        pieces = [own, up, down, far_up, far_down]
        far = (place + 2) % outer * group_spans
        bases = [
            place * group_spans,
            (place + 3) % outer * group_spans,
            (place + 1) % outer * group_spans,
            jnp.where(place >= 2, far, -1),
            jnp.where(place < 2, far, -1),
        ]
    else:
        pieces = [lax.all_gather(own, "outer", axis=0, tiled=True)]
        bases = [jnp.int32(0)]
    out = attention(q, pieces, bases, place * group_spans, span_order)
    out = lax.all_to_all(out.reshape(KVH, rows, GROUP * HD), GROUP_AXES, split_axis=0, concat_axis=0, tiled=False)
    return out.transpose(1, 0, 2).reshape(rows, HQ * HD)


def solution(mesh):
    ctx, head = mesh.devices.shape
    inner = KVH // head
    split = Mesh(mesh.devices.reshape(ctx // inner, inner, head), ("outer", "inner", "head"))
    spec = P(("outer", "inner", "head"), None)
    return jax.shard_map(
        functools.partial(shards, ctx // inner),
        mesh=split,
        in_specs=(spec, spec, spec, P()),
        out_specs=spec,
        check_vma=False,
    )
```

```python
import functools
import math

import jax
import jax.numpy as jnp
from jax import lax
from jax.experimental import pallas as pl
from jax.experimental.pallas import tpu as pltpu
from jax.sharding import Mesh
from jax.sharding import PartitionSpec as P

HQ = 64
KVH = 8
HD = 128
SPAN = 128
GROUP = HQ // KVH
ROWS = GROUP * SPAN
SCALE = HD**-0.5 * math.log2(math.e)
EXTRA = 16
BLOCK = 4
NT = (((1,), (1,)), ((), ()))
GROUP_AXES = ("inner", "head")


def queries_of(q_ref):
    return jnp.concatenate([q_ref[:, g * HD : (g + 1) * HD] for g in range(GROUP)], 0)


def scores(keys, q_ref):
    return lax.dot_general(keys, queries_of(q_ref), NT, preferred_element_type=jnp.float32) * SCALE


def blend(values, weights):
    ones = jnp.ones((EXTRA, values.shape[1]), jnp.bfloat16)
    values = jnp.concatenate([values, ones], 0)
    return jnp.dot(values, weights.astype(jnp.bfloat16), preferred_element_type=jnp.float32)


def causal(s):
    key = lax.broadcasted_iota(jnp.int32, (SPAN, ROWS), 0)
    row = lax.broadcasted_iota(jnp.int32, (SPAN, ROWS), 1) % SPAN
    return jnp.where(key <= row, s, -1e30)


def gather(kv_ref, slots):
    return (
        jnp.concatenate([kv_ref[s, :SPAN] for s in slots], 0),
        jnp.concatenate([kv_ref[s, SPAN:] for s in slots], 1),
    )


def list_spans(order_ref, slot_ref, list_ref, rank_ref, wanted):
    spans = order_ref.shape[0]

    def invert(j, carry):
        slot_ref[order_ref[j]] = j
        return carry

    lax.fori_loop(0, spans, invert, 0)

    def take(t, count):
        j = slot_ref[t]
        rank_ref[t] = count
        list_ref[count] = j
        return count + jnp.where(wanted(j), 1, 0)

    lax.fori_loop(0, spans, take, jnp.int32(0))


def near_kernel(n_kv, *refs):
    where_ref, order_ref, q_ref = refs[:3]
    kv_refs = refs[3 : 3 + n_kv]
    acc_ref, m_ref, kv_ref, slot_ref, list_ref, rank_ref = refs[3 + n_kv :]
    step = pl.program_id(0)

    @pl.when(step == 0)
    def _():
        first = where_ref[1]
        last = first + where_ref[2]
        list_spans(order_ref, slot_ref, list_ref, rank_ref, lambda j: jnp.logical_or(j < first, j >= last))
        for index, piece_ref in enumerate(kv_refs):
            for j in range(piece_ref.shape[0]):
                kv_ref[where_ref[3 + index] + j] = piece_ref[j]

    rank = rank_ref[order_ref[where_ref[0] + step]]

    def first_block(count):
        keys, values = gather(kv_ref, [list_ref[rank + 1 - count + t] for t in range(count)])
        s = scores(keys, q_ref)
        own = causal(s[(count - 1) * SPAN :])
        s = jnp.concatenate([s[: (count - 1) * SPAN], own], 0) if count > 1 else own
        m = jnp.max(s, axis=0, keepdims=True)
        m_ref[0] = jnp.broadcast_to(m, m_ref.shape[1:])
        acc_ref[0] = blend(values, jnp.exp2(s - m))

    for count in range(1, BLOCK + 1):

        @pl.when(rank % BLOCK == count - 1)
        def _(count=count):
            first_block(count)

    def block(b, carry):
        keys, values = gather(kv_ref, [list_ref[b * BLOCK + t] for t in range(BLOCK)])
        acc_ref[0] += blend(values, jnp.exp2(scores(keys, q_ref) - m_ref[0, :1]))
        return carry

    lax.fori_loop(0, rank // BLOCK, block, 0)


def far_kernel(n_kv, n_far, *refs):
    where_ref, order_ref, q_ref, acc_in, m_in = refs[:5]
    kv_refs = refs[5 : 5 + n_kv]
    o_ref, acc_ref, run_ref, kv_ref, slot_ref, list_ref, rank_ref = refs[5 + n_kv :]
    step = pl.program_id(0)
    first = where_ref[1]
    last = first + where_ref[2]

    @pl.when(step == 0)
    def _():
        list_spans(order_ref, slot_ref, list_ref, rank_ref, lambda j: jnp.logical_and(j >= first, j < last))
        for index in range(n_kv - n_far, n_kv):

            @pl.when(where_ref[3 + index] >= 0)
            def _(piece_ref=kv_refs[index]):
                for j in range(piece_ref.shape[0]):
                    kv_ref[j] = piece_ref[j]

    p = order_ref[where_ref[0] + step]
    acc_ref[...] = acc_in[0]
    if n_far:
        count = rank_ref[p]

        def block(start, size):
            keys, values = gather(kv_ref, [list_ref[start + t] - first for t in range(size)])
            acc_ref[...] += blend(values, jnp.exp2(scores(keys, q_ref) - m_in[0, :1]))

        def whole(b, carry):
            block(b * BLOCK, BLOCK)
            return carry

        lax.fori_loop(0, count // BLOCK, whole, 0)
        for size in range(1, BLOCK):

            @pl.when(count % BLOCK == size)
            def _(size=size):
                block(count - size, size)

    @pl.when(jnp.logical_not(jnp.max(acc_ref[HD : HD + 8]) < 1e30))
    def _():
        run_ref[...] = jnp.full_like(run_ref, -1e30)
        acc_ref[...] = jnp.zeros_like(acc_ref)
        for index, piece_ref in enumerate(kv_refs):
            base = where_ref[3 + index]

            def careful(j, carry, piece_ref=piece_ref, base=base):
                other = order_ref[jnp.maximum(base, 0) + j]

                @pl.when(jnp.logical_and(base >= 0, other <= p))
                def _():
                    s = scores(piece_ref[j, :SPAN], q_ref)
                    s = jnp.where(other < p, s, causal(s))
                    old = run_ref[...]
                    new = jnp.maximum(old, jnp.max(s, axis=0, keepdims=True))
                    run_ref[...] = new
                    fresh = blend(piece_ref[j, SPAN:], jnp.exp2(s - new[:1]))
                    acc_ref[...] = acc_ref[...] * jnp.exp2(old - new)[:1] + fresh

                return carry

            lax.fori_loop(0, piece_ref.shape[0], careful, 0)

    result = acc_ref[:HD] * (1.0 / acc_ref[HD : HD + 1])
    for g in range(GROUP):
        o_ref[:, g * HD : (g + 1) * HD] = result[:, g * SPAN : (g + 1) * SPAN].T.astype(o_ref.dtype)


def attention(q, near, far, near_bases, far_bases, far_first, far_count, first_span, span_order):
    q_spans = q.shape[0] // SPAN
    spans = span_order.shape[0]
    where = jnp.stack([first_span, far_first, far_count, *near_bases, *far_bases]).astype(jnp.int32)
    q_spec = pl.BlockSpec((SPAN, GROUP * HD), lambda i, *_: (i, 0))
    acc_spec = pl.BlockSpec((1, HD + EXTRA, ROWS), lambda i, *_: (i, 0, 0))
    m_spec = pl.BlockSpec((1, 8, ROWS), lambda i, *_: (i, 0, 0))
    piece_specs = [pl.BlockSpec(piece.shape, lambda i, *_: (0, 0, 0)) for piece in near + far]
    lists = [pltpu.SMEM((spans,), jnp.int32)] * 3
    elements = q.shape[0] * GROUP * spans * SPAN // 2
    limit = pltpu.CompilerParams(vmem_limit_bytes=40 * 2**20)

    def cost(part):
        return pl.CostEstimate(
            flops=int(8 * HD * elements * part),
            bytes_accessed=4 * q.size + 4 * spans * SPAN * HD,
            transcendentals=int(elements * part),
        )

    acc, m = pl.pallas_call(
        functools.partial(near_kernel, len(near)),
        grid_spec=pltpu.PrefetchScalarGridSpec(
            num_scalar_prefetch=2,
            grid=(q_spans,),
            in_specs=[q_spec] + piece_specs[: len(near)],
            out_specs=[acc_spec, m_spec],
            scratch_shapes=[pltpu.VMEM((spans, SPAN + HD, SPAN), jnp.bfloat16), *lists],
        ),
        out_shape=[
            jax.ShapeDtypeStruct((q_spans, HD + EXTRA, ROWS), jnp.float32),
            jax.ShapeDtypeStruct((q_spans, 8, ROWS), jnp.float32),
        ],
        compiler_params=limit,
        cost_estimate=cost(0.75),
        name="near",
    )(where, span_order, q, *near)
    return pl.pallas_call(
        functools.partial(far_kernel, len(near) + len(far), len(far)),
        grid_spec=pltpu.PrefetchScalarGridSpec(
            num_scalar_prefetch=2,
            grid=(q_spans,),
            in_specs=[q_spec, acc_spec, m_spec] + piece_specs,
            out_specs=q_spec,
            scratch_shapes=[
                pltpu.VMEM((HD + EXTRA, ROWS), jnp.float32),
                pltpu.VMEM((8, ROWS), jnp.float32),
                pltpu.VMEM((near[0].shape[0], SPAN + HD, SPAN), jnp.bfloat16),
                *lists,
            ],
        ),
        out_shape=jax.ShapeDtypeStruct(q.shape, q.dtype),
        compiler_params=limit,
        cost_estimate=cost(0.25),
        name="far",
    )(where, span_order, q, acc, m, *near, *far)


def pack_kernel(k_ref, v_ref, o_ref):
    for h in range(KVH):
        o_ref[h, :SPAN] = k_ref[:, h * HD : (h + 1) * HD]
        o_ref[h, SPAN:] = v_ref[:, h * HD : (h + 1) * HD].T


def to_head_owners(key_rows, value_rows):
    rows = key_rows.shape[0]
    exchange = functools.partial(
        lax.all_to_all, axis_name=GROUP_AXES, split_axis=0, concat_axis=0, tiled=False
    )
    if rows == SPAN:
        packed = pl.pallas_call(
            pack_kernel, out_shape=jax.ShapeDtypeStruct((KVH, SPAN + HD, SPAN), key_rows.dtype), name="pack"
        )(key_rows, value_rows)
        return exchange(packed)
    packed = jnp.concatenate([key_rows.reshape(rows, KVH, HD), value_rows.reshape(rows, KVH, HD)], 2)
    own = exchange(packed.transpose(1, 0, 2)).reshape(KVH * rows // SPAN, SPAN, 2 * HD)
    return jnp.concatenate([own[:, :, :HD], own[:, :, HD:].transpose(0, 2, 1)], 1)


def shards(outer, queries, key_rows, value_rows, span_order):
    rows = queries.shape[0]
    place = lax.axis_index("outer")
    group_rows = KVH * rows
    group_spans = group_rows // SPAN
    own = to_head_owners(key_rows, value_rows)
    q = queries.reshape(rows, KVH, GROUP * HD).transpose(1, 0, 2)
    q = lax.all_to_all(q, GROUP_AXES, split_axis=0, concat_axis=0, tiled=False).reshape(group_rows, GROUP * HD)
    if outer == 4:
        up = lax.ppermute(own, "outer", [(i, (i + 1) % outer) for i in range(outer)])
        down = lax.ppermute(own, "outer", [(i, (i - 1) % outer) for i in range(outer)])
        far_up = lax.ppermute(up, "outer", [(1, 2), (2, 3)])
        far_down = lax.ppermute(down, "outer", [(1, 0), (2, 1)])
        near = [own, up, down]
        near_bases = [(place + step) % outer * group_spans for step in (0, outer - 1, 1)]
        far = [far_up, far_down]
        far_first = (place + 2) % outer * group_spans
        far_count = jnp.int32(group_spans)
        far_bases = [jnp.where(place >= 2, far_first, -1), jnp.where(place < 2, far_first, -1)]
    else:
        near = [lax.all_gather(own, "outer", axis=0, tiled=True)]
        near_bases = [jnp.int32(0)]
        far, far_bases, far_first, far_count = [], [], jnp.int32(0), jnp.int32(0)
    out = attention(q, near, far, near_bases, far_bases, far_first, far_count, place * group_spans, span_order)
    out = lax.all_to_all(out.reshape(KVH, rows, GROUP * HD), GROUP_AXES, split_axis=0, concat_axis=0, tiled=False)
    return out.transpose(1, 0, 2).reshape(rows, HQ * HD)


def solution(mesh):
    ctx, head = mesh.devices.shape
    inner = KVH // head
    split = Mesh(mesh.devices.reshape(ctx // inner, inner, head), ("outer", "inner", "head"))
    spec = P(("outer", "inner", "head"), None)
    return jax.shard_map(
        functools.partial(shards, ctx // inner),
        mesh=split,
        in_specs=(spec, spec, spec, P()),
        out_specs=spec,
        check_vma=False,
    )
```

```python
import functools
import math

import jax
import jax.numpy as jnp
from jax import lax
from jax.experimental import pallas as pl
from jax.experimental.pallas import tpu as pltpu
from jax.sharding import Mesh
from jax.sharding import PartitionSpec as P

HQ = 64
KVH = 8
HD = 128
SPAN = 128
GROUP = HQ // KVH
ROWS = GROUP * SPAN
SCALE = HD**-0.5 * math.log2(math.e)
EXTRA = 16
BLOCK = 4
NT = (((1,), (1,)), ((), ()))
GROUP_AXES = ("inner", "head")
PARTS = ((5, 7, 1, 4), (3, 6, 2, 0))


def queries_of(q_ref):
    return jnp.concatenate([q_ref[:, g * HD : (g + 1) * HD] for g in range(GROUP)], 0)


def scores(keys, q_ref):
    return lax.dot_general(keys, queries_of(q_ref), NT, preferred_element_type=jnp.float32) * SCALE


def blend(values, weights):
    ones = jnp.ones((EXTRA, values.shape[1]), jnp.bfloat16)
    values = jnp.concatenate([values, ones], 0)
    return jnp.dot(values, weights.astype(jnp.bfloat16), preferred_element_type=jnp.float32)


def causal(s):
    key = lax.broadcasted_iota(jnp.int32, (SPAN, ROWS), 0)
    row = lax.broadcasted_iota(jnp.int32, (SPAN, ROWS), 1) % SPAN
    return jnp.where(key <= row, s, -1e30)


def gather(kv_ref, slots):
    return (
        jnp.concatenate([kv_ref[s, :SPAN] for s in slots], 0),
        jnp.concatenate([kv_ref[s, SPAN:] for s in slots], 1),
    )


def list_spans(order_ref, slot_ref, list_ref, rank_ref, wanted):
    spans = order_ref.shape[0]

    def invert(j, carry):
        slot_ref[order_ref[j]] = j
        return carry

    lax.fori_loop(0, spans, invert, 0)

    def take(t, count):
        j = slot_ref[t]
        rank_ref[t] = count
        list_ref[count] = j
        return count + jnp.where(wanted(j), 1, 0)

    lax.fori_loop(0, spans, take, jnp.int32(0))


def near_kernel(n_kv, *refs):
    where_ref, order_ref, q_ref = refs[:3]
    kv_refs = refs[3 : 3 + n_kv]
    acc_ref, m_ref, kv_ref, slot_ref, list_ref, rank_ref = refs[3 + n_kv :]
    step = pl.program_id(0)

    @pl.when(step == 0)
    def _():
        first = where_ref[1]
        last = first + where_ref[2]
        list_spans(order_ref, slot_ref, list_ref, rank_ref, lambda j: jnp.logical_or(j < first, j >= last))
        for index, piece_ref in enumerate(kv_refs):
            for j in range(piece_ref.shape[0]):
                kv_ref[where_ref[3 + index] + j] = piece_ref[j]

    rank = rank_ref[order_ref[where_ref[0] + step]]

    def first_block(count):
        keys, values = gather(kv_ref, [list_ref[rank + 1 - count + t] for t in range(count)])
        s = scores(keys, q_ref)
        own = causal(s[(count - 1) * SPAN :])
        s = jnp.concatenate([s[: (count - 1) * SPAN], own], 0) if count > 1 else own
        m = jnp.max(s, axis=0, keepdims=True)
        m_ref[0] = jnp.broadcast_to(m, m_ref.shape[1:])
        acc_ref[0] = blend(values, jnp.exp2(s - m))

    for count in range(1, BLOCK + 1):

        @pl.when(rank % BLOCK == count - 1)
        def _(count=count):
            first_block(count)

    def block(b, carry):
        keys, values = gather(kv_ref, [list_ref[b * BLOCK + t] for t in range(BLOCK)])
        acc_ref[0] += blend(values, jnp.exp2(scores(keys, q_ref) - m_ref[0, :1]))
        return carry

    lax.fori_loop(0, rank // BLOCK, block, 0)


def far_kernel(n_kv, n_far, n_out, *refs):
    where_ref, order_ref, sequence_ref, q_ref, acc_in, m_in = refs[:6]
    kv_refs = refs[6 : 6 + n_kv]
    o_refs = refs[6 + n_kv : 6 + n_kv + n_out]
    acc_ref, run_ref, kv_ref, slot_ref, list_ref, rank_ref = refs[6 + n_kv + n_out :]
    step = pl.program_id(0)
    first = where_ref[1]
    last = first + where_ref[2]

    @pl.when(step == 0)
    def _():
        list_spans(order_ref, slot_ref, list_ref, rank_ref, lambda j: jnp.logical_and(j >= first, j < last))
        for index in range(n_kv - n_far, n_kv):

            @pl.when(where_ref[3 + index] >= 0)
            def _(piece_ref=kv_refs[index]):
                for j in range(piece_ref.shape[0]):
                    kv_ref[j] = piece_ref[j]

    p = order_ref[where_ref[0] + sequence_ref[step]]
    acc_ref[...] = acc_in[0]
    if n_far:
        count = rank_ref[p]

        def block(start, size):
            keys, values = gather(kv_ref, [list_ref[start + t] - first for t in range(size)])
            acc_ref[...] += blend(values, jnp.exp2(scores(keys, q_ref) - m_in[0, :1]))

        def whole(b, carry):
            block(b * BLOCK, BLOCK)
            return carry

        lax.fori_loop(0, count // BLOCK, whole, 0)
        for size in range(1, BLOCK):

            @pl.when(count % BLOCK == size)
            def _(size=size):
                block(count - size, size)

    @pl.when(jnp.logical_not(jnp.max(acc_ref[HD : HD + 8]) < 1e30))
    def _():
        run_ref[...] = jnp.full_like(run_ref, -1e30)
        acc_ref[...] = jnp.zeros_like(acc_ref)
        for index, piece_ref in enumerate(kv_refs):
            base = where_ref[3 + index]

            def careful(j, carry, piece_ref=piece_ref, base=base):
                other = order_ref[jnp.maximum(base, 0) + j]

                @pl.when(jnp.logical_and(base >= 0, other <= p))
                def _():
                    s = scores(piece_ref[j, :SPAN], q_ref)
                    s = jnp.where(other < p, s, causal(s))
                    old = run_ref[...]
                    new = jnp.maximum(old, jnp.max(s, axis=0, keepdims=True))
                    run_ref[...] = new
                    fresh = blend(piece_ref[j, SPAN:], jnp.exp2(s - new[:1]))
                    acc_ref[...] = acc_ref[...] * jnp.exp2(old - new)[:1] + fresh

                return carry

            lax.fori_loop(0, piece_ref.shape[0], careful, 0)

    for index, o_ref in enumerate(o_refs):

        @pl.when(jnp.logical_or(n_out == 1, step == index))
        def _(o_ref=o_ref):
            result = acc_ref[:HD] * (1.0 / acc_ref[HD : HD + 1])
            for g in range(GROUP):
                o_ref[:, g * HD : (g + 1) * HD] = result[:, g * SPAN : (g + 1) * SPAN].T.astype(o_ref.dtype)


def attention(q, near, far, near_bases, far_bases, far_first, far_count, first_span, span_order):
    q_spans = q.shape[0] // SPAN
    spans = span_order.shape[0]
    where = jnp.stack([first_span, far_first, far_count, *near_bases, *far_bases]).astype(jnp.int32)
    q_spec = pl.BlockSpec((SPAN, GROUP * HD), lambda i, *_: (i, 0))
    acc_spec = pl.BlockSpec((1, HD + EXTRA, ROWS), lambda i, *_: (i, 0, 0))
    m_spec = pl.BlockSpec((1, 8, ROWS), lambda i, *_: (i, 0, 0))
    piece_specs = [pl.BlockSpec(piece.shape, lambda i, *_: (0, 0, 0)) for piece in near + far]
    lists = [pltpu.SMEM((spans,), jnp.int32)] * 3
    elements = q.shape[0] * GROUP * spans * SPAN // 2
    limit = pltpu.CompilerParams(vmem_limit_bytes=40 * 2**20)

    def cost(part):
        return pl.CostEstimate(
            flops=int(8 * HD * elements * part),
            bytes_accessed=4 * q.size + 4 * spans * SPAN * HD,
            transcendentals=int(elements * part),
        )

    acc, m = pl.pallas_call(
        functools.partial(near_kernel, len(near)),
        grid_spec=pltpu.PrefetchScalarGridSpec(
            num_scalar_prefetch=2,
            grid=(q_spans,),
            in_specs=[q_spec] + piece_specs[: len(near)],
            out_specs=[acc_spec, m_spec],
            scratch_shapes=[pltpu.VMEM((spans, SPAN + HD, SPAN), jnp.bfloat16), *lists],
        ),
        out_shape=[
            jax.ShapeDtypeStruct((q_spans, HD + EXTRA, ROWS), jnp.float32),
            jax.ShapeDtypeStruct((q_spans, 8, ROWS), jnp.float32),
        ],
        compiler_params=limit,
        cost_estimate=cost(0.75),
        name="near",
    )(where, span_order, q, *near)

    def finish(sequence, count, apart):
        q_block = pl.BlockSpec((SPAN, GROUP * HD), lambda i, w, o, seq: (seq[i], 0))
        acc_block = pl.BlockSpec((1, HD + EXTRA, ROWS), lambda i, w, o, seq: (seq[i], 0, 0))
        m_block = pl.BlockSpec((1, 8, ROWS), lambda i, w, o, seq: (seq[i], 0, 0))
        if apart:
            out_specs = [pl.BlockSpec((SPAN, GROUP * HD), lambda i, *_: (0, 0))] * count
            out_shape = [jax.ShapeDtypeStruct((SPAN, GROUP * HD), q.dtype)] * count
        else:
            out_specs, out_shape = [q_block], [jax.ShapeDtypeStruct(q.shape, q.dtype)]
        return pl.pallas_call(
            functools.partial(far_kernel, len(near) + len(far), len(far), len(out_shape)),
            grid_spec=pltpu.PrefetchScalarGridSpec(
                num_scalar_prefetch=3,
                grid=(count,),
                in_specs=[q_block, acc_block, m_block] + piece_specs,
                out_specs=out_specs,
                scratch_shapes=[
                    pltpu.VMEM((HD + EXTRA, ROWS), jnp.float32),
                    pltpu.VMEM((8, ROWS), jnp.float32),
                    pltpu.VMEM((near[0].shape[0], SPAN + HD, SPAN), jnp.bfloat16),
                    *lists,
                ],
            ),
            out_shape=out_shape,
            compiler_params=limit,
            cost_estimate=cost(0.25 * count / q_spans),
            name="far",
        )(where, span_order, sequence, q, acc, m, *near, *far)

    return finish


def unpack_kernel(me_ref, *refs):
    o_ref = refs[-1]
    for index, part_ref in enumerate(refs[:-1]):
        column = pl.multiple_of((me_ref[0] ^ index) * GROUP * HD, GROUP * HD)
        o_ref[:, pl.ds(column, GROUP * HD)] = part_ref[...]


def to_token_owners(finish, q_spans):
    me = lax.axis_index(GROUP_AXES)
    parts = [None] * KVH
    for steps in PARTS:
        sequence = jnp.stack([me ^ step for step in steps]).astype(jnp.int32)
        for step, done in zip(steps, finish(sequence, len(steps), True)):
            if step:
                done = lax.ppermute(done, GROUP_AXES, [(i, i ^ step) for i in range(KVH)])
            parts[step] = done
    return pl.pallas_call(
        unpack_kernel,
        grid_spec=pltpu.PrefetchScalarGridSpec(
            num_scalar_prefetch=1,
            grid=(1,),
            in_specs=[pl.BlockSpec((SPAN, GROUP * HD), lambda i, *_: (0, 0))] * KVH,
            out_specs=pl.BlockSpec((SPAN, HQ * HD), lambda i, *_: (0, 0)),
        ),
        out_shape=jax.ShapeDtypeStruct((SPAN, HQ * HD), parts[0].dtype),
        name="unpack",
    )(me.reshape(1).astype(jnp.int32), *parts)


def pack_kernel(k_ref, v_ref, o_ref):
    for h in range(KVH):
        o_ref[h, :SPAN] = k_ref[:, h * HD : (h + 1) * HD]
        o_ref[h, SPAN:] = v_ref[:, h * HD : (h + 1) * HD].T


def to_head_owners(key_rows, value_rows):
    rows = key_rows.shape[0]
    exchange = functools.partial(
        lax.all_to_all, axis_name=GROUP_AXES, split_axis=0, concat_axis=0, tiled=False
    )
    if rows == SPAN:
        packed = pl.pallas_call(
            pack_kernel, out_shape=jax.ShapeDtypeStruct((KVH, SPAN + HD, SPAN), key_rows.dtype), name="pack"
        )(key_rows, value_rows)
        return exchange(packed)
    packed = jnp.concatenate([key_rows.reshape(rows, KVH, HD), value_rows.reshape(rows, KVH, HD)], 2)
    own = exchange(packed.transpose(1, 0, 2)).reshape(KVH * rows // SPAN, SPAN, 2 * HD)
    return jnp.concatenate([own[:, :, :HD], own[:, :, HD:].transpose(0, 2, 1)], 1)


def shards(outer, queries, key_rows, value_rows, span_order):
    rows = queries.shape[0]
    place = lax.axis_index("outer")
    group_rows = KVH * rows
    group_spans = group_rows // SPAN
    own = to_head_owners(key_rows, value_rows)
    q = queries.reshape(rows, KVH, GROUP * HD).transpose(1, 0, 2)
    q = lax.all_to_all(q, GROUP_AXES, split_axis=0, concat_axis=0, tiled=False).reshape(group_rows, GROUP * HD)
    if outer == 4:
        up = lax.ppermute(own, "outer", [(i, (i + 1) % outer) for i in range(outer)])
        down = lax.ppermute(own, "outer", [(i, (i - 1) % outer) for i in range(outer)])
        far_up = lax.ppermute(up, "outer", [(1, 2), (2, 3)])
        far_down = lax.ppermute(down, "outer", [(1, 0), (2, 1)])
        near = [own, up, down]
        near_bases = [(place + step) % outer * group_spans for step in (0, outer - 1, 1)]
        far = [far_up, far_down]
        far_first = (place + 2) % outer * group_spans
        far_count = jnp.int32(group_spans)
        far_bases = [jnp.where(place >= 2, far_first, -1), jnp.where(place < 2, far_first, -1)]
    else:
        near = [lax.all_gather(own, "outer", axis=0, tiled=True)]
        near_bases = [jnp.int32(0)]
        far, far_bases, far_first, far_count = [], [], jnp.int32(0), jnp.int32(0)
    finish = attention(q, near, far, near_bases, far_bases, far_first, far_count, place * group_spans, span_order)
    if rows == SPAN:
        return to_token_owners(finish, group_spans)
    out = finish(jnp.arange(group_spans, dtype=jnp.int32), group_spans, False)[0]
    out = lax.all_to_all(out.reshape(KVH, rows, GROUP * HD), GROUP_AXES, split_axis=0, concat_axis=0, tiled=False)
    return out.transpose(1, 0, 2).reshape(rows, HQ * HD)


def solution(mesh):
    ctx, head = mesh.devices.shape
    inner = KVH // head
    split = Mesh(mesh.devices.reshape(ctx // inner, inner, head), ("outer", "inner", "head"))
    spec = P(("outer", "inner", "head"), None)
    return jax.shard_map(
        functools.partial(shards, ctx // inner),
        mesh=split,
        in_specs=(spec, spec, spec, P()),
        out_specs=spec,
        check_vma=False,
    )
```

```python
import functools
import math

import jax
import jax.numpy as jnp
from jax import lax
from jax.experimental import pallas as pl
from jax.experimental.pallas import tpu as pltpu
from jax.sharding import Mesh
from jax.sharding import PartitionSpec as P

HQ = 64
KVH = 8
HD = 128
SPAN = 128
GROUP = HQ // KVH
ROWS = GROUP * SPAN
SCALE = HD**-0.5 * math.log2(math.e)
EXTRA = 16
BLOCK = 8
VMEM = 24 * 2**20
NT = (((1,), (1,)), ((), ()))
GROUP_AXES = ("inner", "head")
PARTS = ((5, 7), (1, 4, 3), (6, 2, 0))


def queries_of(q_ref):
    return jnp.concatenate([q_ref[:, g * HD : (g + 1) * HD] for g in range(GROUP)], 0)


def scores(keys, q_ref):
    return lax.dot_general(keys, queries_of(q_ref), NT, preferred_element_type=jnp.float32) * SCALE


def blend(values, weights):
    ones = jnp.ones((EXTRA, values.shape[1]), jnp.bfloat16)
    values = jnp.concatenate([values, ones], 0)
    return jnp.dot(values, weights.astype(jnp.bfloat16), preferred_element_type=jnp.float32)


def causal(s):
    key = lax.broadcasted_iota(jnp.int32, (SPAN, ROWS), 0)
    row = lax.broadcasted_iota(jnp.int32, (SPAN, ROWS), 1) % SPAN
    return jnp.where(key <= row, s, -1e30)


def gather(kv_ref, slots):
    return (
        jnp.concatenate([kv_ref[s, :SPAN] for s in slots], 0),
        jnp.concatenate([kv_ref[s, SPAN:] for s in slots], 1),
    )


def listing(order, wanted):
    n = order.shape[0]
    numbers = jnp.arange(n, dtype=jnp.int32)
    before = jnp.logical_and(order[None, :] < order[:, None], wanted[None, :])
    rank = jnp.sum(before.astype(jnp.int32), axis=1)
    mine = jnp.logical_and(rank[None, :] == numbers[:, None], wanted[None, :])
    return rank, jnp.sum(jnp.where(mine, numbers[None, :], 0), axis=1)


class Table:
    def __init__(self, spans):
        self.first, self.far_first, self.bases = 0, 1, 2
        self.order = 16
        self.near_rank, self.near_list, self.far_rank, self.far_list = (16 + spans * (1 + t) for t in range(4))
        self.sequence = 16 + spans * 5


def near_kernel(at, n_kv, *refs):
    t_ref, q_ref = refs[:2]
    pieces = refs[2 : 2 + n_kv]
    acc_ref, m_ref, kv_ref, sems = refs[2 + n_kv :]
    step = pl.program_id(0)

    @pl.when(step == 0)
    def _():
        copies = [
            pltpu.make_async_copy(
                piece, kv_ref.at[pl.ds(t_ref[at.bases + index], piece.shape[0])], sems.at[index]
            )
            for index, piece in enumerate(pieces)
        ]
        for copy in copies:
            copy.start()
        for copy in copies:
            copy.wait()

    rank = t_ref[at.near_rank + t_ref[at.first] + step]

    def first_block(count):
        start = at.near_list + rank + 1 - count
        keys, values = gather(kv_ref, [t_ref[start + t] for t in range(count)])
        s = scores(keys, q_ref)
        own = causal(s[(count - 1) * SPAN :])
        s = jnp.concatenate([s[: (count - 1) * SPAN], own], 0) if count > 1 else own
        m = jnp.max(s, axis=0, keepdims=True)
        m_ref[0] = jnp.broadcast_to(m, m_ref.shape[1:])
        acc_ref[0] = blend(values, jnp.exp2(s - m))

    for count in range(1, BLOCK + 1):

        @pl.when(rank % BLOCK == count - 1)
        def _(count=count):
            first_block(count)

    def block(b, carry):
        keys, values = gather(kv_ref, [t_ref[at.near_list + b * BLOCK + t] for t in range(BLOCK)])
        acc_ref[0] += blend(values, jnp.exp2(scores(keys, q_ref) - m_ref[0, :1]))
        return carry

    lax.fori_loop(0, rank // BLOCK, block, 0)


def far_kernel(at, offset, n_kv, n_far, n_out, *refs):
    t_ref, q_ref, acc_in, m_in = refs[:4]
    pieces = refs[4 : 4 + n_kv]
    o_refs = refs[4 + n_kv : 4 + n_kv + n_out]
    acc_ref, run_ref, kv_ref, span_ref, sem = refs[4 + n_kv + n_out :]
    step = pl.program_id(0)
    stored = t_ref[at.first] + t_ref[at.sequence + offset + step]
    p = t_ref[at.order + stored]

    @pl.when(step == 0)
    def _():
        for index in range(n_kv - n_far, n_kv):

            @pl.when(t_ref[at.bases + index] >= 0)
            def _(piece=pieces[index]):
                copy = pltpu.make_async_copy(piece, kv_ref, sem)
                copy.start()
                copy.wait()

    count = t_ref[at.far_rank + stored] if n_far else 0

    @pl.when(count == 0)
    def _():
        acc_ref[...] = acc_in[0]

    for size in range(1, 1 + (kv_ref.shape[0] if n_far else 0)):

        @pl.when(count == size)
        def _(size=size):
            slots = [t_ref[at.far_list + t] - t_ref[at.far_first] for t in range(size)]
            keys, values = gather(kv_ref, slots)
            acc_ref[...] = acc_in[0] + blend(values, jnp.exp2(scores(keys, q_ref) - m_in[0, :1]))

    @pl.when(jnp.logical_not(jnp.max(acc_ref[HD : HD + 8]) < 1e30))
    def _():
        run_ref[...] = jnp.full_like(run_ref, -1e30)
        acc_ref[...] = jnp.zeros_like(acc_ref)
        for index, piece in enumerate(pieces):
            base = t_ref[at.bases + index]

            def careful(j, carry, piece=piece, base=base):
                other = t_ref[at.order + jnp.maximum(base, 0) + j]

                @pl.when(jnp.logical_and(base >= 0, other <= p))
                def _():
                    copy = pltpu.make_async_copy(piece.at[j], span_ref, sem)
                    copy.start()
                    copy.wait()
                    s = scores(span_ref[:SPAN], q_ref)
                    s = jnp.where(other < p, s, causal(s))
                    old = run_ref[...]
                    new = jnp.maximum(old, jnp.max(s, axis=0, keepdims=True))
                    run_ref[...] = new
                    fresh = blend(span_ref[SPAN:], jnp.exp2(s - new[:1]))
                    acc_ref[...] = acc_ref[...] * jnp.exp2(old - new)[:1] + fresh

                return carry

            lax.fori_loop(0, piece.shape[0], careful, 0)

    for index, o_ref in enumerate(o_refs):

        @pl.when(jnp.logical_or(n_out == 1, step == index))
        def _(o_ref=o_ref):
            result = acc_ref[:HD] * (1.0 / acc_ref[HD : HD + 1])
            for g in range(GROUP):
                o_ref[:, g * HD : (g + 1) * HD] = result[:, g * SPAN : (g + 1) * SPAN].T.astype(o_ref.dtype)


def attention(q, near, far, near_bases, far_bases, far_first, first_span, span_order, sequence):
    q_spans = q.shape[0] // SPAN
    spans = span_order.shape[0]
    at = Table(spans)
    numbers = jnp.arange(spans, dtype=jnp.int32)
    if far:
        is_far = jnp.logical_and(numbers >= far_first, numbers < far_first + far[0].shape[0])
    else:
        is_far = numbers < 0
    head = jnp.stack([first_span, far_first, *near_bases, *far_bases]).astype(jnp.int32)
    head = jnp.pad(head, (0, at.order - head.shape[0]))
    near_lists = listing(span_order, jnp.logical_not(is_far))
    table = jnp.concatenate([head, span_order, *near_lists, *listing(span_order, is_far), sequence])
    elements = q.shape[0] * GROUP * spans * SPAN // 2
    limit = pltpu.CompilerParams(vmem_limit_bytes=VMEM)
    anywhere = pl.BlockSpec(memory_space=pl.ANY)

    def cost(part):
        return pl.CostEstimate(
            flops=int(8 * HD * elements * part),
            bytes_accessed=4 * q.size + 4 * spans * SPAN * HD,
            transcendentals=int(elements * part),
        )

    acc, m = pl.pallas_call(
        functools.partial(near_kernel, at, len(near)),
        grid_spec=pltpu.PrefetchScalarGridSpec(
            num_scalar_prefetch=1,
            grid=(q_spans,),
            in_specs=[pl.BlockSpec((SPAN, GROUP * HD), lambda i, t: (i, 0))] + [anywhere] * len(near),
            out_specs=[
                pl.BlockSpec((1, HD + EXTRA, ROWS), lambda i, t: (i, 0, 0)),
                pl.BlockSpec((1, 8, ROWS), lambda i, t: (i, 0, 0)),
            ],
            scratch_shapes=[
                pltpu.VMEM((spans, SPAN + HD, SPAN), jnp.bfloat16),
                pltpu.SemaphoreType.DMA((len(near),)),
            ],
        ),
        out_shape=[
            jax.ShapeDtypeStruct((q_spans, HD + EXTRA, ROWS), jnp.float32),
            jax.ShapeDtypeStruct((q_spans, 8, ROWS), jnp.float32),
        ],
        compiler_params=limit,
        cost_estimate=cost(0.75),
        name="near",
    )(table, q, *near)

    def finish(offset, count, apart):
        def nth(i, t):
            return t[at.sequence + offset + i]

        q_block = pl.BlockSpec((SPAN, GROUP * HD), lambda i, t: (nth(i, t), 0))
        acc_block = pl.BlockSpec((1, HD + EXTRA, ROWS), lambda i, t: (nth(i, t), 0, 0))
        m_block = pl.BlockSpec((1, 8, ROWS), lambda i, t: (nth(i, t), 0, 0))
        if apart:
            out_specs = [pl.BlockSpec((SPAN, GROUP * HD), lambda i, t: (0, 0))] * count
            out_shape = [jax.ShapeDtypeStruct((SPAN, GROUP * HD), q.dtype)] * count
        else:
            out_specs, out_shape = [q_block], [jax.ShapeDtypeStruct(q.shape, q.dtype)]
        n_kv = len(near) + len(far)
        return pl.pallas_call(
            functools.partial(far_kernel, at, offset, n_kv, len(far), len(out_shape)),
            grid_spec=pltpu.PrefetchScalarGridSpec(
                num_scalar_prefetch=1,
                grid=(count,),
                in_specs=[q_block, acc_block, m_block] + [anywhere] * n_kv,
                out_specs=out_specs,
                scratch_shapes=[
                    pltpu.VMEM((HD + EXTRA, ROWS), jnp.float32),
                    pltpu.VMEM((8, ROWS), jnp.float32),
                    pltpu.VMEM((near[0].shape[0], SPAN + HD, SPAN), jnp.bfloat16),
                    pltpu.VMEM((SPAN + HD, SPAN), jnp.bfloat16),
                    pltpu.SemaphoreType.DMA,
                ],
            ),
            out_shape=out_shape,
            compiler_params=limit,
            cost_estimate=cost(0.25 * count / q_spans),
            name="far",
        )(table, q, acc, m, *near, *far)

    return finish


def unpack_kernel(me_ref, *refs):
    o_ref = refs[-1]
    for index, part_ref in enumerate(refs[:-1]):
        column = pl.multiple_of((me_ref[0] ^ index) * GROUP * HD, GROUP * HD)
        o_ref[:, pl.ds(column, GROUP * HD)] = part_ref[...]


def to_token_owners(finish, me):
    parts = [None] * KVH
    offset = 0
    for steps in PARTS:
        for step, done in zip(steps, finish(offset, len(steps), True)):
            if step:
                done = lax.ppermute(done, GROUP_AXES, [(i, i ^ step) for i in range(KVH)])
            parts[step] = done
        offset += len(steps)
    return pl.pallas_call(
        unpack_kernel,
        grid_spec=pltpu.PrefetchScalarGridSpec(
            num_scalar_prefetch=1,
            grid=(1,),
            in_specs=[pl.BlockSpec((SPAN, GROUP * HD), lambda i, *_: (0, 0))] * KVH,
            out_specs=pl.BlockSpec((SPAN, HQ * HD), lambda i, *_: (0, 0)),
        ),
        out_shape=jax.ShapeDtypeStruct((SPAN, HQ * HD), parts[0].dtype),
        compiler_params=pltpu.CompilerParams(vmem_limit_bytes=VMEM),
        name="unpack",
    )(me.reshape(1), *parts)


def pack_kernel(k_ref, v_ref, o_ref):
    for h in range(KVH):
        o_ref[h, :SPAN] = k_ref[:, h * HD : (h + 1) * HD]
        o_ref[h, SPAN:] = v_ref[:, h * HD : (h + 1) * HD].T


def to_head_owners(key_rows, value_rows):
    rows = key_rows.shape[0]
    exchange = functools.partial(
        lax.all_to_all, axis_name=GROUP_AXES, split_axis=0, concat_axis=0, tiled=False
    )
    if rows == SPAN:
        packed = pl.pallas_call(
            pack_kernel, out_shape=jax.ShapeDtypeStruct((KVH, SPAN + HD, SPAN), key_rows.dtype), name="pack",
            compiler_params=pltpu.CompilerParams(vmem_limit_bytes=VMEM),
        )(key_rows, value_rows)
        return exchange(packed)
    packed = jnp.concatenate([key_rows.reshape(rows, KVH, HD), value_rows.reshape(rows, KVH, HD)], 2)
    own = exchange(packed.transpose(1, 0, 2)).reshape(KVH * rows // SPAN, SPAN, 2 * HD)
    return jnp.concatenate([own[:, :, :HD], own[:, :, HD:].transpose(0, 2, 1)], 1)


def shards(outer, queries, key_rows, value_rows, span_order):
    rows = queries.shape[0]
    place = lax.axis_index("outer")
    group_rows = KVH * rows
    group_spans = group_rows // SPAN
    own = to_head_owners(key_rows, value_rows)
    q = queries.reshape(rows, KVH, GROUP * HD).transpose(1, 0, 2)
    q = lax.all_to_all(q, GROUP_AXES, split_axis=0, concat_axis=0, tiled=False).reshape(group_rows, GROUP * HD)
    if outer == 4:
        up = lax.ppermute(own, "outer", [(i, (i + 1) % outer) for i in range(outer)])
        down = lax.ppermute(own, "outer", [(i, (i - 1) % outer) for i in range(outer)])
        far_up = lax.ppermute(up, "outer", [(1, 2), (2, 3)])
        far_down = lax.ppermute(down, "outer", [(1, 0), (2, 1)])
        near = [own, up, down]
        near_bases = [(place + step) % outer * group_spans for step in (0, outer - 1, 1)]
        far = [far_up, far_down]
        far_first = (place + 2) % outer * group_spans
        far_bases = [jnp.where(place >= 2, far_first, -1), jnp.where(place < 2, far_first, -1)]
    else:
        near = [lax.all_gather(own, "outer", axis=0, tiled=True)]
        near_bases = [jnp.int32(0)]
        far, far_bases, far_first = [], [], jnp.int32(0)
    me = lax.axis_index(GROUP_AXES).astype(jnp.int32)
    if rows == SPAN:
        sequence = jnp.stack([me ^ step for steps in PARTS for step in steps])
    else:
        sequence = jnp.arange(group_spans, dtype=jnp.int32)
    finish = attention(q, near, far, near_bases, far_bases, far_first, place * group_spans, span_order, sequence)
    if rows == SPAN:
        return to_token_owners(finish, me)
    out = finish(0, group_spans, False)[0]
    out = lax.all_to_all(out.reshape(KVH, rows, GROUP * HD), GROUP_AXES, split_axis=0, concat_axis=0, tiled=False)
    return out.transpose(1, 0, 2).reshape(rows, HQ * HD)


def solution(mesh):
    ctx, head = mesh.devices.shape
    inner = KVH // head
    split = Mesh(mesh.devices.reshape(ctx // inner, inner, head), ("outer", "inner", "head"))
    spec = P(("outer", "inner", "head"), None)
    return jax.shard_map(
        functools.partial(shards, ctx // inner),
        mesh=split,
        in_specs=(spec, spec, spec, P()),
        out_specs=spec,
        check_vma=False,
    )
```

```python
import functools
import math

import jax
import jax.numpy as jnp
from jax import lax
from jax.experimental import pallas as pl
from jax.experimental.pallas import tpu as pltpu
from jax.sharding import Mesh
from jax.sharding import PartitionSpec as P

HQ = 64
KVH = 8
HD = 128
SPAN = 128
GROUP = HQ // KVH
ROWS = GROUP * SPAN
SCALE = HD**-0.5 * math.log2(math.e)
EXTRA = 16
BLOCK = 8
VMEM = 24 * 2**20
NT = (((1,), (1,)), ((), ()))
GROUP_AXES = ("inner", "head")
PARTS = (((5, 7), (1, 4, 3, 6)), ((2, 0),))


def queries_of(q_ref):
    return jnp.concatenate([q_ref[:, g * HD : (g + 1) * HD] for g in range(GROUP)], 0)


def scores(keys, q_ref):
    return lax.dot_general(keys, queries_of(q_ref), NT, preferred_element_type=jnp.float32) * SCALE


def blend(values, weights):
    ones = jnp.ones((EXTRA, values.shape[1]), jnp.bfloat16)
    values = jnp.concatenate([values, ones], 0)
    return jnp.dot(values, weights.astype(jnp.bfloat16), preferred_element_type=jnp.float32)


def causal(s):
    key = lax.broadcasted_iota(jnp.int32, (SPAN, ROWS), 0)
    row = lax.broadcasted_iota(jnp.int32, (SPAN, ROWS), 1) % SPAN
    return jnp.where(key <= row, s, -1e30)


def gather(kv_ref, slots):
    return (
        jnp.concatenate([kv_ref[s, :SPAN] for s in slots], 0),
        jnp.concatenate([kv_ref[s, SPAN:] for s in slots], 1),
    )


def listing(order, wanted):
    n = order.shape[0]
    numbers = jnp.arange(n, dtype=jnp.int32)
    before = jnp.logical_and(order[None, :] < order[:, None], wanted[None, :])
    rank = jnp.sum(before.astype(jnp.int32), axis=1)
    mine = jnp.logical_and(rank[None, :] == numbers[:, None], wanted[None, :])
    return rank, jnp.sum(jnp.where(mine, numbers[None, :], 0), axis=1)


class Table:
    def __init__(self, spans):
        self.first, self.far_first, self.bases = 0, 1, 2
        self.order = 16
        self.near_rank, self.near_list, self.far_rank, self.far_list = (16 + spans * (1 + t) for t in range(4))
        self.sequence = 16 + spans * 5


def near_kernel(at, offset, n_kv, *refs):
    t_ref, q_ref = refs[:2]
    pieces = refs[2 : 2 + n_kv]
    acc_ref, m_ref, kv_ref, sems = refs[2 + n_kv :]
    step = pl.program_id(0)

    @pl.when(step == 0)
    def _():
        copies = [
            pltpu.make_async_copy(
                piece, kv_ref.at[pl.ds(t_ref[at.bases + index], piece.shape[0])], sems.at[index]
            )
            for index, piece in enumerate(pieces)
        ]
        for copy in copies:
            copy.start()
        for copy in copies:
            copy.wait()

    rank = t_ref[at.near_rank + t_ref[at.first] + t_ref[at.sequence + offset + step]]

    def first_block(count):
        others = [t_ref[at.near_list + rank - t] for t in range(1, count)]
        keys, values = gather(kv_ref, [t_ref[at.near_list + rank], *others])
        s = scores(keys, q_ref)
        own = causal(s[:SPAN])
        m = jnp.max(own, axis=0, keepdims=True)
        s = jnp.concatenate([own, s[SPAN:]], 0) if count > 1 else own
        m_ref[0] = jnp.broadcast_to(m, m_ref.shape[1:])
        acc_ref[0] = blend(values, jnp.exp2(s - m))

    for count in range(1, BLOCK + 1):

        @pl.when(rank % BLOCK == count - 1)
        def _(count=count):
            first_block(count)

    def block(b, carry):
        keys, values = gather(kv_ref, [t_ref[at.near_list + b * BLOCK + t] for t in range(BLOCK)])
        acc_ref[0] += blend(values, jnp.exp2(scores(keys, q_ref) - m_ref[0, :1]))
        return carry

    lax.fori_loop(0, rank // BLOCK, block, 0)


def far_kernel(at, offset, n_kv, n_far, n_out, *refs):
    t_ref, q_ref, acc_in, m_in = refs[:4]
    pieces = refs[4 : 4 + n_kv]
    o_refs = refs[4 + n_kv : 4 + n_kv + n_out]
    acc_ref, run_ref, kv_ref, span_ref, sem = refs[4 + n_kv + n_out :]
    step = pl.program_id(0)
    stored = t_ref[at.first] + t_ref[at.sequence + offset + step]
    p = t_ref[at.order + stored]

    @pl.when(step == 0)
    def _():
        for index in range(n_kv - n_far, n_kv):

            @pl.when(t_ref[at.bases + index] >= 0)
            def _(piece=pieces[index]):
                copy = pltpu.make_async_copy(piece, kv_ref, sem)
                copy.start()
                copy.wait()

    count = t_ref[at.far_rank + stored] if n_far else 0

    @pl.when(count == 0)
    def _():
        acc_ref[...] = acc_in[0]

    for size in range(1, 1 + (kv_ref.shape[0] if n_far else 0)):

        @pl.when(count == size)
        def _(size=size):
            slots = [t_ref[at.far_list + t] - t_ref[at.far_first] for t in range(size)]
            keys, values = gather(kv_ref, slots)
            acc_ref[...] = acc_in[0] + blend(values, jnp.exp2(scores(keys, q_ref) - m_in[0, :1]))

    @pl.when(jnp.logical_not(jnp.max(acc_ref[HD : HD + 8]) < 1e30))
    def _():
        run_ref[...] = jnp.full_like(run_ref, -1e30)
        acc_ref[...] = jnp.zeros_like(acc_ref)
        for index, piece in enumerate(pieces):
            base = t_ref[at.bases + index]

            def careful(j, carry, piece=piece, base=base):
                other = t_ref[at.order + jnp.maximum(base, 0) + j]

                @pl.when(jnp.logical_and(base >= 0, other <= p))
                def _():
                    copy = pltpu.make_async_copy(piece.at[j], span_ref, sem)
                    copy.start()
                    copy.wait()
                    s = scores(span_ref[:SPAN], q_ref)
                    s = jnp.where(other < p, s, causal(s))
                    old = run_ref[...]
                    new = jnp.maximum(old, jnp.max(s, axis=0, keepdims=True))
                    run_ref[...] = new
                    fresh = blend(span_ref[SPAN:], jnp.exp2(s - new[:1]))
                    acc_ref[...] = acc_ref[...] * jnp.exp2(old - new)[:1] + fresh

                return carry

            lax.fori_loop(0, piece.shape[0], careful, 0)

    for index, o_ref in enumerate(o_refs):

        @pl.when(jnp.logical_or(n_out == 1, step == index))
        def _(o_ref=o_ref):
            result = acc_ref[:HD] * (1.0 / acc_ref[HD : HD + 1])
            for g in range(GROUP):
                o_ref[:, g * HD : (g + 1) * HD] = result[:, g * SPAN : (g + 1) * SPAN].T.astype(o_ref.dtype)


def attention(q, near, far, near_bases, far_bases, far_first, first_span, span_order, sequence):
    q_spans = q.shape[0] // SPAN
    spans = span_order.shape[0]
    at = Table(spans)
    numbers = jnp.arange(spans, dtype=jnp.int32)
    if far:
        is_far = jnp.logical_and(numbers >= far_first, numbers < far_first + far[0].shape[0])
    else:
        is_far = numbers < 0
    head = jnp.stack([first_span, far_first, *near_bases, *far_bases]).astype(jnp.int32)
    head = jnp.pad(head, (0, at.order - head.shape[0]))
    near_lists = listing(span_order, jnp.logical_not(is_far))
    table = jnp.concatenate([head, span_order, *near_lists, *listing(span_order, is_far), sequence])
    elements = q.shape[0] * GROUP * spans * SPAN // 2
    limit = pltpu.CompilerParams(vmem_limit_bytes=VMEM)
    anywhere = pl.BlockSpec(memory_space=pl.ANY)

    def cost(part):
        return pl.CostEstimate(
            flops=int(8 * HD * elements * part),
            bytes_accessed=4 * q.size + 4 * spans * SPAN * HD,
            transcendentals=int(elements * part),
        )

    def begin(offset, count, q):
        return pl.pallas_call(
            functools.partial(near_kernel, at, offset, len(near)),
            grid_spec=pltpu.PrefetchScalarGridSpec(
                num_scalar_prefetch=1,
                grid=(count,),
                in_specs=[pl.BlockSpec((SPAN, GROUP * HD), lambda i, t: (t[at.sequence + offset + i], 0))]
                + [anywhere] * len(near),
                out_specs=[
                    pl.BlockSpec((1, HD + EXTRA, ROWS), lambda i, t: (i, 0, 0)),
                    pl.BlockSpec((1, 8, ROWS), lambda i, t: (i, 0, 0)),
                ],
                scratch_shapes=[
                    pltpu.VMEM((spans, SPAN + HD, SPAN), jnp.bfloat16),
                    pltpu.SemaphoreType.DMA((len(near),)),
                ],
            ),
            out_shape=[
                jax.ShapeDtypeStruct((count, HD + EXTRA, ROWS), jnp.float32),
                jax.ShapeDtypeStruct((count, 8, ROWS), jnp.float32),
            ],
            compiler_params=limit,
            cost_estimate=cost(0.75 * count / q_spans),
            name="near",
        )(table, q, *near)

    def finish(begun, begun_at, offset, count, apart):
        skip = offset - begun_at

        def nth(i, t):
            return t[at.sequence + offset + i]

        q_block = pl.BlockSpec((SPAN, GROUP * HD), lambda i, t: (nth(i, t), 0))
        acc_block = pl.BlockSpec((1, HD + EXTRA, ROWS), lambda i, t: (skip + i, 0, 0))
        m_block = pl.BlockSpec((1, 8, ROWS), lambda i, t: (skip + i, 0, 0))
        if apart:
            out_specs = [pl.BlockSpec((SPAN, GROUP * HD), lambda i, t: (0, 0))] * count
            out_shape = [jax.ShapeDtypeStruct((SPAN, GROUP * HD), q.dtype)] * count
        else:
            out_specs, out_shape = [q_block], [jax.ShapeDtypeStruct(q.shape, q.dtype)]
        n_kv = len(near) + len(far)
        return pl.pallas_call(
            functools.partial(far_kernel, at, offset, n_kv, len(far), len(out_shape)),
            grid_spec=pltpu.PrefetchScalarGridSpec(
                num_scalar_prefetch=1,
                grid=(count,),
                in_specs=[q_block, acc_block, m_block] + [anywhere] * n_kv,
                out_specs=out_specs,
                scratch_shapes=[
                    pltpu.VMEM((HD + EXTRA, ROWS), jnp.float32),
                    pltpu.VMEM((8, ROWS), jnp.float32),
                    pltpu.VMEM((near[0].shape[0], SPAN + HD, SPAN), jnp.bfloat16),
                    pltpu.VMEM((SPAN + HD, SPAN), jnp.bfloat16),
                    pltpu.SemaphoreType.DMA,
                ],
            ),
            out_shape=out_shape,
            compiler_params=limit,
            cost_estimate=cost(0.25 * count / q_spans),
            name="far",
        )(table, q, *begun, *near, *far)

    return begin, finish


def unpack_kernel(me_ref, *refs):
    o_ref = refs[-1]
    for index, part_ref in enumerate(refs[:-1]):
        column = pl.multiple_of((me_ref[0] ^ index) * GROUP * HD, GROUP * HD)
        o_ref[:, pl.ds(column, GROUP * HD)] = part_ref[...]


def to_token_owners(q, begin, finish, me):
    parts = [None] * KVH
    offset = 0
    for together in PARTS:
        begun_at = offset
        begun = begin(offset, sum(map(len, together)), q)
        for steps in together:
            finished = finish(begun, begun_at, offset, len(steps), True)
            offset += len(steps)
            for step, done in zip(steps, finished):
                if step:
                    parts[step] = lax.ppermute(done, GROUP_AXES, [(i, i ^ step) for i in range(KVH)])
                else:
                    parts[step] = done
        q, _ = lax.optimization_barrier((q, (finished, [parts[step] for step in together[0]])))
    return pl.pallas_call(
        unpack_kernel,
        grid_spec=pltpu.PrefetchScalarGridSpec(
            num_scalar_prefetch=1,
            grid=(1,),
            in_specs=[pl.BlockSpec((SPAN, GROUP * HD), lambda i, *_: (0, 0))] * KVH,
            out_specs=pl.BlockSpec((SPAN, HQ * HD), lambda i, *_: (0, 0)),
        ),
        out_shape=jax.ShapeDtypeStruct((SPAN, HQ * HD), parts[0].dtype),
        compiler_params=pltpu.CompilerParams(vmem_limit_bytes=VMEM),
        name="unpack",
    )(me.reshape(1), *parts)


def pack_kernel(k_ref, v_ref, o_ref):
    for h in range(KVH):
        o_ref[h, :SPAN] = k_ref[:, h * HD : (h + 1) * HD]
        o_ref[h, SPAN:] = v_ref[:, h * HD : (h + 1) * HD].T


def to_head_owners(key_rows, value_rows):
    rows = key_rows.shape[0]
    exchange = functools.partial(
        lax.all_to_all, axis_name=GROUP_AXES, split_axis=0, concat_axis=0, tiled=False
    )
    if rows == SPAN:
        packed = pl.pallas_call(
            pack_kernel, out_shape=jax.ShapeDtypeStruct((KVH, SPAN + HD, SPAN), key_rows.dtype), name="pack"
        )(key_rows, value_rows)
        return exchange(packed)
    packed = jnp.concatenate([key_rows.reshape(rows, KVH, HD), value_rows.reshape(rows, KVH, HD)], 2)
    own = exchange(packed.transpose(1, 0, 2)).reshape(KVH * rows // SPAN, SPAN, 2 * HD)
    return jnp.concatenate([own[:, :, :HD], own[:, :, HD:].transpose(0, 2, 1)], 1)


def shards(outer, queries, key_rows, value_rows, span_order):
    rows = queries.shape[0]
    place = lax.axis_index("outer")
    group_rows = KVH * rows
    group_spans = group_rows // SPAN
    own = to_head_owners(key_rows, value_rows)
    q = queries.reshape(rows, KVH, GROUP * HD).transpose(1, 0, 2)
    q = lax.all_to_all(q, GROUP_AXES, split_axis=0, concat_axis=0, tiled=False).reshape(group_rows, GROUP * HD)
    if outer == 4:
        up = lax.ppermute(own, "outer", [(i, (i + 1) % outer) for i in range(outer)])
        down = lax.ppermute(own, "outer", [(i, (i - 1) % outer) for i in range(outer)])
        far_up = lax.ppermute(up, "outer", [(1, 2), (2, 3)])
        far_down = lax.ppermute(down, "outer", [(1, 0), (2, 1)])
        near = [own, up, down]
        near_bases = [(place + step) % outer * group_spans for step in (0, outer - 1, 1)]
        far = [far_up, far_down]
        far_first = (place + 2) % outer * group_spans
        far_bases = [jnp.where(place >= 2, far_first, -1), jnp.where(place < 2, far_first, -1)]
    else:
        near = [lax.all_gather(own, "outer", axis=0, tiled=True)]
        near_bases = [jnp.int32(0)]
        far, far_bases, far_first = [], [], jnp.int32(0)
    me = lax.axis_index(GROUP_AXES).astype(jnp.int32)
    if rows == SPAN:
        sequence = jnp.stack([me ^ step for together in PARTS for steps in together for step in steps])
    else:
        sequence = jnp.arange(group_spans, dtype=jnp.int32)
    begin, finish = attention(q, near, far, near_bases, far_bases, far_first, place * group_spans, span_order, sequence)
    if rows == SPAN:
        return to_token_owners(q, begin, finish, me)
    out = finish(begin(0, group_spans, q), 0, 0, group_spans, False)[0]
    out = lax.all_to_all(out.reshape(KVH, rows, GROUP * HD), GROUP_AXES, split_axis=0, concat_axis=0, tiled=False)
    return out.transpose(1, 0, 2).reshape(rows, HQ * HD)


def solution(mesh):
    ctx, head = mesh.devices.shape
    inner = KVH // head
    split = Mesh(mesh.devices.reshape(ctx // inner, inner, head), ("outer", "inner", "head"))
    spec = P(("outer", "inner", "head"), None)
    return jax.shard_map(
        functools.partial(shards, ctx // inner),
        mesh=split,
        in_specs=(spec, spec, spec, P()),
        out_specs=spec,
        check_vma=False,
    )
```

```python
import functools
import math

import jax
import jax.numpy as jnp
from jax import lax
from jax.experimental import pallas as pl
from jax.experimental.pallas import tpu as pltpu
from jax.sharding import Mesh
from jax.sharding import PartitionSpec as P

HQ = 64
KVH = 8
HD = 128
SPAN = 128
GROUP = HQ // KVH
ROWS = GROUP * SPAN
SCALE = HD**-0.5 * math.log2(math.e)
EXTRA = 16
BLOCK = 8
VMEM = 24 * 2**20
NT = (((1,), (1,)), ((), ()))
GROUP_AXES = ("inner", "head")
AWAY = ((5, 7), (1, 4, 3, 6))
HOME = (2, 0)


def queries_of(q_ref):
    return jnp.concatenate([q_ref[:, g * HD : (g + 1) * HD] for g in range(GROUP)], 0)


def scores(keys, q_ref):
    return lax.dot_general(keys, queries_of(q_ref), NT, preferred_element_type=jnp.float32) * SCALE


def blend(values, weights):
    ones = jnp.ones((EXTRA, values.shape[1]), jnp.bfloat16)
    values = jnp.concatenate([values, ones], 0)
    return jnp.dot(values, weights.astype(jnp.bfloat16), preferred_element_type=jnp.float32)


def causal(s):
    key = lax.broadcasted_iota(jnp.int32, (SPAN, ROWS), 0)
    row = lax.broadcasted_iota(jnp.int32, (SPAN, ROWS), 1) % SPAN
    return jnp.where(key <= row, s, -1e30)


def gather(kv_ref, slots):
    return (
        jnp.concatenate([kv_ref[s, :SPAN] for s in slots], 0),
        jnp.concatenate([kv_ref[s, SPAN:] for s in slots], 1),
    )


def listing(order, wanted):
    n = order.shape[0]
    numbers = jnp.arange(n, dtype=jnp.int32)
    before = jnp.logical_and(order[None, :] < order[:, None], wanted[None, :])
    rank = jnp.sum(before.astype(jnp.int32), axis=1)
    mine = jnp.logical_and(rank[None, :] == numbers[:, None], wanted[None, :])
    return rank, jnp.sum(jnp.where(mine, numbers[None, :], 0), axis=1)


class Table:
    def __init__(self, spans):
        self.first, self.far_first, self.bases = 0, 1, 2
        self.order = 16
        self.near_rank, self.near_list, self.far_rank, self.far_list, self.all_list = (
            16 + spans * (1 + t) for t in range(5)
        )
        self.sequence = 16 + spans * 6


def fetch(at, t_ref, pieces, indices, target_of, sems, optional):
    def copy_of(index):
        return pltpu.make_async_copy(pieces[index], target_of(index), sems.at[index])

    for act in ("start", "wait"):
        for index in indices:
            if index in optional:

                @pl.when(t_ref[at.bases + index] >= 0)
                def _(index=index):
                    getattr(copy_of(index), act)()

            else:
                getattr(copy_of(index), act)()


def attend(t_ref, list_at, rank, q_ref, kv_ref, acc_ref, m_ref):
    def first_block(count):
        others = [t_ref[list_at + rank - t] for t in range(1, count)]
        keys, values = gather(kv_ref, [t_ref[list_at + rank], *others])
        s = scores(keys, q_ref)
        own = causal(s[:SPAN])
        m = jnp.max(own, axis=0, keepdims=True)
        s = jnp.concatenate([own, s[SPAN:]], 0) if count > 1 else own
        m_ref[...] = jnp.broadcast_to(m, m_ref.shape)
        acc_ref[...] = blend(values, jnp.exp2(s - m))

    for count in range(1, BLOCK + 1):

        @pl.when(rank % BLOCK == count - 1)
        def _(count=count):
            first_block(count)

    def block(b, carry):
        keys, values = gather(kv_ref, [t_ref[list_at + b * BLOCK + t] for t in range(BLOCK)])
        acc_ref[...] += blend(values, jnp.exp2(scores(keys, q_ref) - m_ref[:1]))
        return carry

    lax.fori_loop(0, rank // BLOCK, block, 0)


def recheck(at, t_ref, p, q_ref, pieces, acc_ref, run_ref, span_ref, sem):
    @pl.when(jnp.logical_not(jnp.max(acc_ref[HD : HD + 8]) < 1e30))
    def _():
        run_ref[...] = jnp.full_like(run_ref, -1e30)
        acc_ref[...] = jnp.zeros_like(acc_ref)
        for index, piece in enumerate(pieces):
            base = t_ref[at.bases + index]

            def careful(j, carry, piece=piece, base=base):
                other = t_ref[at.order + jnp.maximum(base, 0) + j]

                @pl.when(jnp.logical_and(base >= 0, other <= p))
                def _():
                    copy = pltpu.make_async_copy(piece.at[j], span_ref, sem)
                    copy.start()
                    copy.wait()
                    s = scores(span_ref[:SPAN], q_ref)
                    s = jnp.where(other < p, s, causal(s))
                    old = run_ref[...]
                    new = jnp.maximum(old, jnp.max(s, axis=0, keepdims=True))
                    run_ref[...] = new
                    fresh = blend(span_ref[SPAN:], jnp.exp2(s - new[:1]))
                    acc_ref[...] = acc_ref[...] * jnp.exp2(old - new)[:1] + fresh

                return carry

            lax.fori_loop(0, piece.shape[0], careful, 0)


def conclude(acc_ref, o_ref):
    result = acc_ref[:HD] * (1.0 / acc_ref[HD : HD + 1])
    for g in range(GROUP):
        o_ref[:, g * HD : (g + 1) * HD] = result[:, g * SPAN : (g + 1) * SPAN].T.astype(o_ref.dtype)


def rows_of(ref, span):
    return ref.at[pl.ds(pl.multiple_of(span * SPAN, SPAN), SPAN)]


def near_kernel(at, offset, n_kv, *refs):
    t_ref, q_ref = refs[:2]
    pieces = refs[2 : 2 + n_kv]
    acc_ref, m_ref, kv_ref, sems = refs[2 + n_kv :]
    fetch(
        at, t_ref, pieces, range(n_kv),
        lambda i: kv_ref.at[pl.ds(t_ref[at.bases + i], pieces[i].shape[0])], sems, (),
    )

    def span(step, carry):
        local = t_ref[at.sequence + offset + step]
        rank = t_ref[at.near_rank + t_ref[at.first] + local]
        attend(t_ref, at.near_list, rank, rows_of(q_ref, local), kv_ref, acc_ref.at[step], m_ref.at[step])
        return carry

    lax.fori_loop(0, acc_ref.shape[0], span, 0)


def far_kernel(at, offset, skip, n_kv, n_far, n_out, *refs):
    t_ref, q_ref, acc_in, m_in = refs[:4]
    pieces = refs[4 : 4 + n_kv]
    o_refs = refs[4 + n_kv : 4 + n_kv + n_out]
    acc_ref, run_ref, kv_ref, span_ref, sems = refs[4 + n_kv + n_out :]
    far = range(n_kv - n_far, n_kv)
    fetch(at, t_ref, pieces, far, lambda i: kv_ref, sems, far)

    def span(step, carry):
        local = t_ref[at.sequence + offset + step]
        stored = t_ref[at.first] + local
        query = rows_of(q_ref, local)
        count = t_ref[at.far_rank + stored]

        @pl.when(count == 0)
        def _():
            acc_ref[...] = acc_in[skip + step]

        for size in range(1, 1 + kv_ref.shape[0]):

            @pl.when(count == size)
            def _(size=size):
                slots = [t_ref[at.far_list + t] - t_ref[at.far_first] for t in range(size)]
                keys, values = gather(kv_ref, slots)
                weights = jnp.exp2(scores(keys, query) - m_in[skip + step, :1])
                acc_ref[...] = acc_in[skip + step] + blend(values, weights)

        recheck(at, t_ref, t_ref[at.order + stored], query, pieces, acc_ref, run_ref, span_ref, sems.at[0])
        for index, o_ref in enumerate(o_refs):

            @pl.when(step == index)
            def _(o_ref=o_ref):
                conclude(acc_ref, o_ref)

        return carry

    lax.fori_loop(0, n_out, span, 0)


def whole_kernel(at, offset, n_kv, n_far, count, *refs):
    t_ref, q_ref = refs[:2]
    pieces = refs[2 : 2 + n_kv]
    o_refs = refs[2 + n_kv : -6]
    acc_ref, m_ref, run_ref, kv_ref, span_ref, sems = refs[-6:]
    fetch(
        at, t_ref, pieces, range(n_kv),
        lambda i: kv_ref.at[pl.ds(t_ref[at.bases + i], pieces[i].shape[0])], sems, range(n_kv - n_far, n_kv),
    )

    def span(step, carry):
        local = t_ref[at.sequence + offset + step]
        p = t_ref[at.order + t_ref[at.first] + local]
        query = rows_of(q_ref, local)
        attend(t_ref, at.all_list, p, query, kv_ref, acc_ref, m_ref)
        recheck(at, t_ref, p, query, pieces, acc_ref, run_ref, span_ref, sems.at[0])
        if len(o_refs) == 1:
            conclude(acc_ref, rows_of(o_refs[0], local))
        else:
            for index, o_ref in enumerate(o_refs):

                @pl.when(step == index)
                def _(o_ref=o_ref):
                    conclude(acc_ref, o_ref)

        return carry

    lax.fori_loop(0, count, span, 0)


def attention(q, near, far, near_bases, far_bases, far_first, first_span, span_order, sequence):
    q_spans = q.shape[0] // SPAN
    spans = span_order.shape[0]
    at = Table(spans)
    numbers = jnp.arange(spans, dtype=jnp.int32)
    if far:
        is_far = jnp.logical_and(numbers >= far_first, numbers < far_first + far[0].shape[0])
    else:
        is_far = numbers < 0
    head = jnp.stack([first_span, far_first, *near_bases, *far_bases]).astype(jnp.int32)
    head = jnp.pad(head, (0, at.order - head.shape[0]))
    near_lists = listing(span_order, jnp.logical_not(is_far))
    far_lists = listing(span_order, is_far)
    all_list = listing(span_order, numbers >= 0)[1]
    table = jnp.concatenate([head, span_order, *near_lists, *far_lists, all_list, sequence])
    elements = q.shape[0] * GROUP * spans * SPAN // 2
    n_kv = len(near) + len(far)
    smem, vmem, anywhere = (pl.BlockSpec(memory_space=space) for space in (pltpu.SMEM, pltpu.VMEM, pl.ANY))
    acc_like = pltpu.VMEM((HD + EXTRA, ROWS), jnp.float32)
    m_like = pltpu.VMEM((8, ROWS), jnp.float32)
    kv_like = pltpu.VMEM((spans, SPAN + HD, SPAN), jnp.bfloat16)
    span_like = pltpu.VMEM((SPAN + HD, SPAN), jnp.bfloat16)

    def call(kernel, name, operands, pieces, out_shape, scratch_shapes, part):
        return pl.pallas_call(
            kernel,
            in_specs=[smem] + [vmem] * (len(operands) - 1) + [anywhere] * len(pieces),
            out_specs=[vmem] * len(out_shape),
            out_shape=out_shape,
            scratch_shapes=[*scratch_shapes, pltpu.SemaphoreType.DMA((n_kv,))],
            compiler_params=pltpu.CompilerParams(vmem_limit_bytes=VMEM),
            cost_estimate=pl.CostEstimate(
                flops=int(8 * HD * elements * part),
                bytes_accessed=int(4 * q.size * part) + 4 * spans * SPAN * HD,
                transcendentals=int(elements * part),
            ),
            name=name,
        )(*operands, *pieces)

    def begin(offset, count, q):
        shapes = [
            jax.ShapeDtypeStruct((count, HD + EXTRA, ROWS), jnp.float32),
            jax.ShapeDtypeStruct((count, 8, ROWS), jnp.float32),
        ]
        kernel = functools.partial(near_kernel, at, offset, len(near))
        return call(kernel, "near", (table, q), near, shapes, [kv_like], 0.75 * count / q_spans)

    def finish(begun, begun_at, offset, count):
        shapes = [jax.ShapeDtypeStruct((SPAN, GROUP * HD), q.dtype)] * count
        kernel = functools.partial(far_kernel, at, offset, offset - begun_at, n_kv, len(far), count)
        scratch = [acc_like, m_like, pltpu.VMEM(far[0].shape, jnp.bfloat16), span_like]
        return call(kernel, "far", (table, q, *begun), near + far, shapes, scratch, 0.25 * count / q_spans)

    def whole(offset, count, q, apart):
        if apart:
            shapes = [jax.ShapeDtypeStruct((SPAN, GROUP * HD), q.dtype)] * count
        else:
            shapes = [jax.ShapeDtypeStruct(q.shape, q.dtype)]
        kernel = functools.partial(whole_kernel, at, offset, n_kv, len(far), count)
        scratch = [acc_like, m_like, m_like, kv_like, span_like]
        return call(kernel, "whole", (table, q), near + far, shapes, scratch, count / q_spans)

    return begin, finish, whole


def unpack_kernel(me_ref, *refs):
    o_ref = refs[-1]
    for index, part_ref in enumerate(refs[:-1]):
        column = pl.multiple_of((me_ref[0] ^ index) * GROUP * HD, GROUP * HD)
        o_ref[:, pl.ds(column, GROUP * HD)] = part_ref[...]


def to_token_owners(q, begin, finish, whole, me):
    parts = [None] * KVH

    def send(steps, finished):
        for step, done in zip(steps, finished):
            if step:
                done = lax.ppermute(done, GROUP_AXES, [(i, i ^ step) for i in range(KVH)])
            parts[step] = done

    begun = begin(0, sum(map(len, AWAY)), q)
    offset = 0
    for steps in AWAY:
        finished = finish(begun, 0, offset, len(steps))
        send(steps, finished)
        offset += len(steps)
    q, _ = lax.optimization_barrier((q, (finished, [parts[step] for step in AWAY[0]])))
    send(HOME, whole(offset, len(HOME), q, True))
    return pl.pallas_call(
        unpack_kernel,
        grid_spec=pltpu.PrefetchScalarGridSpec(
            num_scalar_prefetch=1,
            grid=(1,),
            in_specs=[pl.BlockSpec((SPAN, GROUP * HD), lambda i, *_: (0, 0))] * KVH,
            out_specs=pl.BlockSpec((SPAN, HQ * HD), lambda i, *_: (0, 0)),
        ),
        out_shape=jax.ShapeDtypeStruct((SPAN, HQ * HD), parts[0].dtype),
        compiler_params=pltpu.CompilerParams(vmem_limit_bytes=VMEM),
        name="unpack",
    )(me.reshape(1), *parts)


def pack_kernel(k_ref, v_ref, o_ref):
    for h in range(KVH):
        o_ref[h, :SPAN] = k_ref[:, h * HD : (h + 1) * HD]
        o_ref[h, SPAN:] = v_ref[:, h * HD : (h + 1) * HD].T


def to_head_owners(key_rows, value_rows):
    rows = key_rows.shape[0]
    exchange = functools.partial(
        lax.all_to_all, axis_name=GROUP_AXES, split_axis=0, concat_axis=0, tiled=False
    )
    if rows == SPAN:
        packed = pl.pallas_call(
            pack_kernel, out_shape=jax.ShapeDtypeStruct((KVH, SPAN + HD, SPAN), key_rows.dtype), name="pack"
        )(key_rows, value_rows)
        return exchange(packed)
    packed = jnp.concatenate([key_rows.reshape(rows, KVH, HD), value_rows.reshape(rows, KVH, HD)], 2)
    own = exchange(packed.transpose(1, 0, 2)).reshape(KVH * rows // SPAN, SPAN, 2 * HD)
    return jnp.concatenate([own[:, :, :HD], own[:, :, HD:].transpose(0, 2, 1)], 1)


def shards(outer, queries, key_rows, value_rows, span_order):
    rows = queries.shape[0]
    place = lax.axis_index("outer")
    group_rows = KVH * rows
    group_spans = group_rows // SPAN
    own = to_head_owners(key_rows, value_rows)
    q = queries.reshape(rows, KVH, GROUP * HD).transpose(1, 0, 2)
    q = lax.all_to_all(q, GROUP_AXES, split_axis=0, concat_axis=0, tiled=False).reshape(group_rows, GROUP * HD)
    if outer == 4:
        up = lax.ppermute(own, "outer", [(i, (i + 1) % outer) for i in range(outer)])
        down = lax.ppermute(own, "outer", [(i, (i - 1) % outer) for i in range(outer)])
        far_up = lax.ppermute(up, "outer", [(1, 2), (2, 3)])
        far_down = lax.ppermute(down, "outer", [(1, 0), (2, 1)])
        near = [own, up, down]
        near_bases = [(place + step) % outer * group_spans for step in (0, outer - 1, 1)]
        far = [far_up, far_down]
        far_first = (place + 2) % outer * group_spans
        far_bases = [jnp.where(place >= 2, far_first, -1), jnp.where(place < 2, far_first, -1)]
    else:
        near = [lax.all_gather(own, "outer", axis=0, tiled=True)]
        near_bases = [jnp.int32(0)]
        far, far_bases, far_first = [], [], jnp.int32(0)
    me = lax.axis_index(GROUP_AXES).astype(jnp.int32)
    apart = rows == SPAN and outer == 4
    if apart:
        sequence = jnp.stack([me ^ step for steps in (*AWAY, HOME) for step in steps])
    else:
        sequence = jnp.arange(group_spans, dtype=jnp.int32)
    first_span = place * group_spans
    steps = attention(q, near, far, near_bases, far_bases, far_first, first_span, span_order, sequence)
    if apart:
        return to_token_owners(q, *steps, me)
    out = steps[-1](0, group_spans, q, False)[0]
    out = lax.all_to_all(out.reshape(KVH, rows, GROUP * HD), GROUP_AXES, split_axis=0, concat_axis=0, tiled=False)
    return out.transpose(1, 0, 2).reshape(rows, HQ * HD)


def solution(mesh):
    ctx, head = mesh.devices.shape
    inner = KVH // head
    split = Mesh(mesh.devices.reshape(ctx // inner, inner, head), ("outer", "inner", "head"))
    spec = P(("outer", "inner", "head"), None)
    return jax.shard_map(
        functools.partial(shards, ctx // inner),
        mesh=split,
        in_specs=(spec, spec, spec, P()),
        out_specs=spec,
        check_vma=False,
    )
```

```python
import functools
import math

import jax
import jax.numpy as jnp
from jax import lax
from jax.experimental import pallas as pl
from jax.experimental.pallas import tpu as pltpu
from jax.sharding import Mesh
from jax.sharding import PartitionSpec as P

HQ = 64
KVH = 8
HD = 128
SPAN = 128
GROUP = HQ // KVH
ROWS = GROUP * SPAN
SCALE = HD**-0.5 * math.log2(math.e)
EXTRA = 16
BLOCK = 8
VMEM = 24 * 2**20
NT = (((1,), (1,)), ((), ()))
GROUP_AXES = ("inner", "head")
AWAY = ((5, 7), (1, 4, 3, 6))
HOME = (2, 0)


def queries_of(q_ref):
    return jnp.concatenate([q_ref[:, g * HD : (g + 1) * HD] for g in range(GROUP)], 0)


def scores(keys, q_ref):
    return lax.dot_general(keys, queries_of(q_ref), NT, preferred_element_type=jnp.float32) * SCALE


def blend(values, weights):
    ones = jnp.ones((EXTRA, values.shape[1]), jnp.bfloat16)
    values = jnp.concatenate([values, ones], 0)
    return jnp.dot(values, weights.astype(jnp.bfloat16), preferred_element_type=jnp.float32)


def causal(s):
    key = lax.broadcasted_iota(jnp.int32, (SPAN, ROWS), 0)
    row = lax.broadcasted_iota(jnp.int32, (SPAN, ROWS), 1) % SPAN
    return jnp.where(key <= row, s, -1e30)


def gather(kv_ref, slots):
    return (
        jnp.concatenate([kv_ref[s, :SPAN] for s in slots], 0),
        jnp.concatenate([kv_ref[s, SPAN:] for s in slots], 1),
    )


def listing(order, wanted):
    n = order.shape[0]
    numbers = jnp.arange(n, dtype=jnp.int32)
    before = jnp.logical_and(order[None, :] < order[:, None], wanted[None, :])
    rank = jnp.sum(before.astype(jnp.int32), axis=1)
    mine = jnp.logical_and(rank[None, :] == numbers[:, None], wanted[None, :])
    return rank, jnp.sum(jnp.where(mine, numbers[None, :], 0), axis=1)


class Table:
    def __init__(self, spans):
        self.first, self.far_first, self.bases = 0, 1, 2
        self.order = 16
        self.near_rank, self.near_list, self.far_rank, self.far_list, self.all_list = (
            16 + spans * (1 + t) for t in range(5)
        )
        self.sequence = 16 + spans * 6


def fetch(at, t_ref, pieces, indices, target_of, sems, optional):
    def copy_of(index):
        return pltpu.make_async_copy(pieces[index], target_of(index), sems.at[index])

    for act in ("start", "wait"):
        for index in indices:
            if index in optional:

                @pl.when(t_ref[at.bases + index] >= 0)
                def _(index=index):
                    getattr(copy_of(index), act)()

            else:
                getattr(copy_of(index), act)()


def attend(t_ref, list_at, rank, q_ref, kv_ref, acc_ref, m_ref):
    def first_block(count):
        others = [t_ref[list_at + rank - t] for t in range(1, count)]
        keys, values = gather(kv_ref, [t_ref[list_at + rank], *others])
        s = scores(keys, q_ref)
        own = causal(s[:SPAN])
        m = jnp.max(own, axis=0, keepdims=True)
        s = jnp.concatenate([own, s[SPAN:]], 0) if count > 1 else own
        m_ref[...] = jnp.broadcast_to(m, m_ref.shape)
        acc_ref[...] = blend(values, jnp.exp2(s - m))

    for count in range(1, BLOCK + 1):

        @pl.when(rank % BLOCK == count - 1)
        def _(count=count):
            first_block(count)

    def block(b, carry):
        keys, values = gather(kv_ref, [t_ref[list_at + b * BLOCK + t] for t in range(BLOCK)])
        acc_ref[...] += blend(values, jnp.exp2(scores(keys, q_ref) - m_ref[:1]))
        return carry

    lax.fori_loop(0, rank // BLOCK, block, 0)


def recheck(at, t_ref, p, q_ref, pieces, acc_ref, run_ref, span_ref, sem):
    @pl.when(jnp.logical_not(jnp.max(acc_ref[HD : HD + 8]) < 1e30))
    def _():
        run_ref[...] = jnp.full_like(run_ref, -1e30)
        acc_ref[...] = jnp.zeros_like(acc_ref)
        for index, piece in enumerate(pieces):
            base = t_ref[at.bases + index]

            def careful(j, carry, piece=piece, base=base):
                other = t_ref[at.order + jnp.maximum(base, 0) + j]

                @pl.when(jnp.logical_and(base >= 0, other <= p))
                def _():
                    copy = pltpu.make_async_copy(piece.at[j], span_ref, sem)
                    copy.start()
                    copy.wait()
                    s = scores(span_ref[:SPAN], q_ref)
                    s = jnp.where(other < p, s, causal(s))
                    old = run_ref[...]
                    new = jnp.maximum(old, jnp.max(s, axis=0, keepdims=True))
                    run_ref[...] = new
                    fresh = blend(span_ref[SPAN:], jnp.exp2(s - new[:1]))
                    acc_ref[...] = acc_ref[...] * jnp.exp2(old - new)[:1] + fresh

                return carry

            lax.fori_loop(0, piece.shape[0], careful, 0)


def conclude(acc_ref, o_ref):
    result = acc_ref[:HD] * (1.0 / acc_ref[HD : HD + 1])
    for g in range(GROUP):
        o_ref[:, g * HD : (g + 1) * HD] = result[:, g * SPAN : (g + 1) * SPAN].T.astype(o_ref.dtype)


def rows_of(ref, span):
    return ref.at[pl.ds(pl.multiple_of(span * SPAN, SPAN), SPAN)]


def near_kernel(at, offset, n_kv, *refs):
    t_ref, q_ref = refs[:2]
    pieces = refs[2 : 2 + n_kv]
    acc_ref, m_ref, kv_ref, sems = refs[2 + n_kv :]
    fetch(
        at, t_ref, pieces, range(n_kv),
        lambda i: kv_ref.at[pl.ds(t_ref[at.bases + i], pieces[i].shape[0])], sems, (),
    )

    def span(step, carry):
        local = t_ref[at.sequence + offset + step]
        rank = t_ref[at.near_rank + t_ref[at.first] + local]
        attend(t_ref, at.near_list, rank, rows_of(q_ref, local), kv_ref, acc_ref.at[step], m_ref.at[step])
        return carry

    lax.fori_loop(0, acc_ref.shape[0], span, 0)


def far_kernel(at, offset, skip, n_kv, n_far, n_out, *refs):
    t_ref, q_ref, acc_in, m_in = refs[:4]
    pieces = refs[4 : 4 + n_kv]
    o_refs = refs[4 + n_kv : 4 + n_kv + n_out]
    acc_ref, run_ref, kv_ref, span_ref, sems = refs[4 + n_kv + n_out :]
    far = range(n_kv - n_far, n_kv)
    fetch(at, t_ref, pieces, far, lambda i: kv_ref, sems, far)

    def span(step, carry):
        local = t_ref[at.sequence + offset + step]
        stored = t_ref[at.first] + local
        query = rows_of(q_ref, local)
        count = t_ref[at.far_rank + stored]

        @pl.when(count == 0)
        def _():
            acc_ref[...] = acc_in[skip + step]

        for size in range(1, 1 + kv_ref.shape[0]):

            @pl.when(count == size)
            def _(size=size):
                slots = [t_ref[at.far_list + t] - t_ref[at.far_first] for t in range(size)]
                keys, values = gather(kv_ref, slots)
                weights = jnp.exp2(scores(keys, query) - m_in[skip + step, :1])
                acc_ref[...] = acc_in[skip + step] + blend(values, weights)

        recheck(at, t_ref, t_ref[at.order + stored], query, pieces, acc_ref, run_ref, span_ref, sems.at[0])
        for index, o_ref in enumerate(o_refs):

            @pl.when(step == index)
            def _(o_ref=o_ref):
                conclude(acc_ref, o_ref)

        return carry

    lax.fori_loop(0, n_out, span, 0)


def whole_kernel(at, offset, n_kv, n_far, count, *refs):
    t_ref, q_ref = refs[:2]
    pieces = refs[2 : 2 + n_kv]
    o_refs = refs[2 + n_kv : -6]
    acc_ref, m_ref, run_ref, kv_ref, span_ref, sems = refs[-6:]
    fetch(
        at, t_ref, pieces, range(n_kv),
        lambda i: kv_ref.at[pl.ds(t_ref[at.bases + i], pieces[i].shape[0])], sems, range(n_kv - n_far, n_kv),
    )

    def span(step, carry):
        local = t_ref[at.sequence + offset + step]
        p = t_ref[at.order + t_ref[at.first] + local]
        query = rows_of(q_ref, local)
        attend(t_ref, at.all_list, p, query, kv_ref, acc_ref, m_ref)
        recheck(at, t_ref, p, query, pieces, acc_ref, run_ref, span_ref, sems.at[0])
        if len(o_refs) == 1:
            conclude(acc_ref, rows_of(o_refs[0], local))
        else:
            for index, o_ref in enumerate(o_refs):

                @pl.when(step == index)
                def _(o_ref=o_ref):
                    conclude(acc_ref, o_ref)

        return carry

    lax.fori_loop(0, count, span, 0)


def attention(q, near, far, near_bases, far_bases, far_first, first_span, span_order, sequence):
    q_spans = q.shape[0] // SPAN
    spans = span_order.shape[0]
    at = Table(spans)
    numbers = jnp.arange(spans, dtype=jnp.int32)
    if far:
        is_far = jnp.logical_and(numbers >= far_first, numbers < far_first + far[0].shape[0])
    else:
        is_far = numbers < 0
    head = jnp.stack([first_span, far_first, *near_bases, *far_bases]).astype(jnp.int32)
    head = jnp.pad(head, (0, at.order - head.shape[0]))
    near_lists = listing(span_order, jnp.logical_not(is_far))
    far_lists = listing(span_order, is_far)
    all_list = listing(span_order, numbers >= 0)[1]
    table = jnp.concatenate([head, span_order, *near_lists, *far_lists, all_list, sequence])
    elements = q.shape[0] * GROUP * spans * SPAN // 2
    n_kv = len(near) + len(far)
    smem, vmem = (pl.BlockSpec(memory_space=space) for space in (pltpu.SMEM, pltpu.VMEM))
    acc_like = pltpu.VMEM((HD + EXTRA, ROWS), jnp.float32)
    m_like = pltpu.VMEM((8, ROWS), jnp.float32)
    kv_like = pltpu.VMEM((spans, SPAN + HD, SPAN), jnp.bfloat16)
    span_like = pltpu.VMEM((SPAN + HD, SPAN), jnp.bfloat16)

    def call(kernel, name, operands, pieces, out_shape, scratch_shapes, part):
        return pl.pallas_call(
            kernel,
            in_specs=[smem] + [vmem] * (len(operands) - 1 + len(pieces)),
            out_specs=[vmem] * len(out_shape),
            out_shape=out_shape,
            scratch_shapes=[*scratch_shapes, pltpu.SemaphoreType.DMA((n_kv,))],
            compiler_params=pltpu.CompilerParams(vmem_limit_bytes=VMEM),
            cost_estimate=pl.CostEstimate(
                flops=int(8 * HD * elements * part),
                bytes_accessed=int(4 * q.size * part) + 4 * spans * SPAN * HD,
                transcendentals=int(elements * part),
            ),
            name=name,
        )(*operands, *pieces)

    def begin(offset, count, q):
        shapes = [
            jax.ShapeDtypeStruct((count, HD + EXTRA, ROWS), jnp.float32),
            jax.ShapeDtypeStruct((count, 8, ROWS), jnp.float32),
        ]
        kernel = functools.partial(near_kernel, at, offset, len(near))
        return call(kernel, "near", (table, q), near, shapes, [kv_like], 0.75 * count / q_spans)

    def finish(begun, begun_at, offset, count):
        shapes = [jax.ShapeDtypeStruct((SPAN, GROUP * HD), q.dtype)] * count
        kernel = functools.partial(far_kernel, at, offset, offset - begun_at, n_kv, len(far), count)
        scratch = [acc_like, m_like, pltpu.VMEM(far[0].shape, jnp.bfloat16), span_like]
        return call(kernel, "far", (table, q, *begun), near + far, shapes, scratch, 0.25 * count / q_spans)

    def whole(offset, count, q, apart):
        if apart:
            shapes = [jax.ShapeDtypeStruct((SPAN, GROUP * HD), q.dtype)] * count
        else:
            shapes = [jax.ShapeDtypeStruct(q.shape, q.dtype)]
        kernel = functools.partial(whole_kernel, at, offset, n_kv, len(far), count)
        scratch = [acc_like, m_like, m_like, kv_like, span_like]
        return call(kernel, "whole", (table, q), near + far, shapes, scratch, count / q_spans)

    return begin, finish, whole


def unpack_kernel(me_ref, *refs):
    parts, (o_ref, sems) = refs[:-2], refs[-2:]
    copies = []
    for index, part in enumerate(parts):
        column = pl.multiple_of((me_ref[0] ^ index) * GROUP * HD, GROUP * HD)
        copies.append(pltpu.make_async_copy(part, o_ref.at[:, pl.ds(column, GROUP * HD)], sems.at[index]))
    for copy in copies:
        copy.start()
    for copy in copies:
        copy.wait()


def to_token_owners(q, begin, finish, whole, me):
    parts = [None] * KVH

    def send(steps, finished):
        for step, done in zip(steps, finished):
            if step:
                done = lax.ppermute(done, GROUP_AXES, [(i, i ^ step) for i in range(KVH)])
            parts[step] = done

    begun = begin(0, sum(map(len, AWAY)), q)
    offset = 0
    for steps in AWAY:
        finished = finish(begun, 0, offset, len(steps))
        send(steps, finished)
        offset += len(steps)
    q, _ = lax.optimization_barrier((q, (finished, [parts[step] for step in AWAY[0]])))
    send(HOME, whole(offset, len(HOME), q, True))
    return pl.pallas_call(
        unpack_kernel,
        in_specs=[pl.BlockSpec(memory_space=pltpu.SMEM)] + [pl.BlockSpec(memory_space=pltpu.VMEM)] * KVH,
        out_specs=pl.BlockSpec(memory_space=pl.ANY),
        out_shape=jax.ShapeDtypeStruct((SPAN, HQ * HD), parts[0].dtype),
        scratch_shapes=[pltpu.SemaphoreType.DMA((KVH,))],
        compiler_params=pltpu.CompilerParams(vmem_limit_bytes=VMEM),
        name="unpack",
    )(me.reshape(1), *parts)


def pack_kernel(k_ref, v_ref, o_ref):
    for h in range(KVH):
        o_ref[h, :SPAN] = k_ref[:, h * HD : (h + 1) * HD]
        o_ref[h, SPAN:] = v_ref[:, h * HD : (h + 1) * HD].T


def to_head_owners(key_rows, value_rows):
    rows = key_rows.shape[0]
    exchange = functools.partial(
        lax.all_to_all, axis_name=GROUP_AXES, split_axis=0, concat_axis=0, tiled=False
    )
    if rows == SPAN:
        packed = pl.pallas_call(
            pack_kernel, out_shape=jax.ShapeDtypeStruct((KVH, SPAN + HD, SPAN), key_rows.dtype), name="pack"
        )(key_rows, value_rows)
        return exchange(packed)
    packed = jnp.concatenate([key_rows.reshape(rows, KVH, HD), value_rows.reshape(rows, KVH, HD)], 2)
    own = exchange(packed.transpose(1, 0, 2)).reshape(KVH * rows // SPAN, SPAN, 2 * HD)
    return jnp.concatenate([own[:, :, :HD], own[:, :, HD:].transpose(0, 2, 1)], 1)


def shards(outer, queries, key_rows, value_rows, span_order):
    rows = queries.shape[0]
    place = lax.axis_index("outer")
    group_rows = KVH * rows
    group_spans = group_rows // SPAN
    own = to_head_owners(key_rows, value_rows)
    q = queries.reshape(rows, KVH, GROUP * HD).transpose(1, 0, 2)
    q = lax.all_to_all(q, GROUP_AXES, split_axis=0, concat_axis=0, tiled=False).reshape(group_rows, GROUP * HD)
    if outer == 4:
        up = lax.ppermute(own, "outer", [(i, (i + 1) % outer) for i in range(outer)])
        down = lax.ppermute(own, "outer", [(i, (i - 1) % outer) for i in range(outer)])
        far_up = lax.ppermute(up, "outer", [(1, 2), (2, 3)])
        far_down = lax.ppermute(down, "outer", [(1, 0), (2, 1)])
        near = [own, up, down]
        near_bases = [(place + step) % outer * group_spans for step in (0, outer - 1, 1)]
        far = [far_up, far_down]
        far_first = (place + 2) % outer * group_spans
        far_bases = [jnp.where(place >= 2, far_first, -1), jnp.where(place < 2, far_first, -1)]
    else:
        near = [lax.all_gather(own, "outer", axis=0, tiled=True)]
        near_bases = [jnp.int32(0)]
        far, far_bases, far_first = [], [], jnp.int32(0)
    me = lax.axis_index(GROUP_AXES).astype(jnp.int32)
    apart = rows == SPAN and outer == 4
    if apart:
        sequence = jnp.stack([me ^ step for steps in (*AWAY, HOME) for step in steps])
    else:
        sequence = jnp.arange(group_spans, dtype=jnp.int32)
    first_span = place * group_spans
    steps = attention(q, near, far, near_bases, far_bases, far_first, first_span, span_order, sequence)
    if apart:
        return to_token_owners(q, *steps, me)
    out = steps[-1](0, group_spans, q, False)[0]
    out = lax.all_to_all(out.reshape(KVH, rows, GROUP * HD), GROUP_AXES, split_axis=0, concat_axis=0, tiled=False)
    return out.transpose(1, 0, 2).reshape(rows, HQ * HD)


def solution(mesh):
    ctx, head = mesh.devices.shape
    inner = KVH // head
    split = Mesh(mesh.devices.reshape(ctx // inner, inner, head), ("outer", "inner", "head"))
    spec = P(("outer", "inner", "head"), None)
    return jax.shard_map(
        functools.partial(shards, ctx // inner),
        mesh=split,
        in_specs=(spec, spec, spec, P()),
        out_specs=spec,
        check_vma=False,
    )
```

```python
import functools
import math

import jax
import jax.numpy as jnp
from jax import lax
from jax.experimental import pallas as pl
from jax.experimental.pallas import tpu as pltpu
from jax.sharding import Mesh
from jax.sharding import PartitionSpec as P

HQ = 64
KVH = 8
HD = 128
SPAN = 128
GROUP = HQ // KVH
ROWS = GROUP * SPAN
SCALE = HD**-0.5 * math.log2(math.e)
EXTRA = 16
BLOCK = 8
VMEM = 24 * 2**20
NT = (((1,), (1,)), ((), ()))
GROUP_AXES = ("inner", "head")
AWAY = ((5, 7), (1, 4, 3, 6))
HOME = (2, 0)


def queries_of(q_ref):
    return jnp.concatenate([q_ref[:, g * HD : (g + 1) * HD] for g in range(GROUP)], 0)


def scores(keys, q_ref):
    return lax.dot_general(keys, queries_of(q_ref), NT, preferred_element_type=jnp.float32) * SCALE


def blend(values, weights):
    ones = jnp.ones((EXTRA, values.shape[1]), jnp.bfloat16)
    values = jnp.concatenate([values, ones], 0)
    return jnp.dot(values, weights.astype(jnp.bfloat16), preferred_element_type=jnp.float32)


def causal(s):
    key = lax.broadcasted_iota(jnp.int32, (SPAN, ROWS), 0)
    row = lax.broadcasted_iota(jnp.int32, (SPAN, ROWS), 1) % SPAN
    return jnp.where(key <= row, s, -1e30)


def gather(kv_ref, slots):
    return (
        jnp.concatenate([kv_ref[s, :SPAN] for s in slots], 0),
        jnp.concatenate([kv_ref[s, SPAN:] for s in slots], 1),
    )


def listing(order, wanted):
    n = order.shape[0]
    numbers = jnp.arange(n, dtype=jnp.int32)
    before = jnp.logical_and(order[None, :] < order[:, None], wanted[None, :])
    rank = jnp.sum(before.astype(jnp.int32), axis=1)
    mine = jnp.logical_and(rank[None, :] == numbers[:, None], wanted[None, :])
    return rank, jnp.sum(jnp.where(mine, numbers[None, :], 0), axis=1)


class Table:
    def __init__(self, spans):
        self.first, self.far_first, self.bases = 0, 1, 2
        self.order = 16
        self.near_rank, self.near_list, self.far_rank, self.far_list, self.all_list = (
            16 + spans * (1 + t) for t in range(5)
        )
        self.sequence = 16 + spans * 6


def fetch(pieces, targets, sems):
    copies = [
        pltpu.make_async_copy(piece, target, sems.at[index])
        for index, (piece, target) in enumerate(zip(pieces, targets))
    ]
    for copy in copies:
        copy.start()
    for copy in copies:
        copy.wait()


def places(at, t_ref, kv_ref, pieces):
    return [kv_ref.at[pl.ds(t_ref[at.bases + i], piece.shape[0])] for i, piece in enumerate(pieces)]


def attend(t_ref, list_at, rank, q_ref, kv_ref, acc_ref, m_ref):
    def first_block(count):
        others = [t_ref[list_at + rank - t] for t in range(1, count)]
        keys, values = gather(kv_ref, [t_ref[list_at + rank], *others])
        s = scores(keys, q_ref)
        own = causal(s[:SPAN])
        m = jnp.max(own, axis=0, keepdims=True)
        s = jnp.concatenate([own, s[SPAN:]], 0) if count > 1 else own
        m_ref[...] = jnp.broadcast_to(m, m_ref.shape)
        acc_ref[...] = blend(values, jnp.exp2(s - m))

    for count in range(1, BLOCK + 1):

        @pl.when(rank % BLOCK == count - 1)
        def _(count=count):
            first_block(count)

    def block(b, carry):
        keys, values = gather(kv_ref, [t_ref[list_at + b * BLOCK + t] for t in range(BLOCK)])
        acc_ref[...] += blend(values, jnp.exp2(scores(keys, q_ref) - m_ref[:1]))
        return carry

    lax.fori_loop(0, rank // BLOCK, block, 0)


def recheck(at, t_ref, p, q_ref, pieces, acc_ref, run_ref, span_ref, sem):
    @pl.when(jnp.logical_not(jnp.max(acc_ref[HD : HD + 8]) < 1e30))
    def _():
        run_ref[...] = jnp.full_like(run_ref, -1e30)
        acc_ref[...] = jnp.zeros_like(acc_ref)
        for index, piece in enumerate(pieces):
            base = t_ref[at.bases + index]

            def careful(j, carry, piece=piece, base=base):
                other = t_ref[at.order + base + j]

                @pl.when(other <= p)
                def _():
                    copy = pltpu.make_async_copy(piece.at[j], span_ref, sem)
                    copy.start()
                    copy.wait()
                    s = scores(span_ref[:SPAN], q_ref)
                    s = jnp.where(other < p, s, causal(s))
                    old = run_ref[...]
                    new = jnp.maximum(old, jnp.max(s, axis=0, keepdims=True))
                    run_ref[...] = new
                    fresh = blend(span_ref[SPAN:], jnp.exp2(s - new[:1]))
                    acc_ref[...] = acc_ref[...] * jnp.exp2(old - new)[:1] + fresh

                return carry

            lax.fori_loop(0, piece.shape[0], careful, 0)


def conclude(acc_ref, o_ref):
    result = acc_ref[:HD] * (1.0 / acc_ref[HD : HD + 1])
    for g in range(GROUP):
        o_ref[:, g * HD : (g + 1) * HD] = result[:, g * SPAN : (g + 1) * SPAN].T.astype(o_ref.dtype)


def rows_of(ref, span):
    return ref.at[pl.ds(pl.multiple_of(span * SPAN, SPAN), SPAN)]


def near_kernel(at, offset, n_kv, *refs):
    t_ref, q_ref = refs[:2]
    pieces = refs[2 : 2 + n_kv]
    acc_ref, m_ref, kv_ref, sems = refs[2 + n_kv :]
    fetch(pieces, places(at, t_ref, kv_ref, pieces), sems)

    def span(step, carry):
        local = t_ref[at.sequence + offset + step]
        rank = t_ref[at.near_rank + t_ref[at.first] + local]
        attend(t_ref, at.near_list, rank, rows_of(q_ref, local), kv_ref, acc_ref.at[step], m_ref.at[step])
        return carry

    lax.fori_loop(0, acc_ref.shape[0], span, 0)


def far_kernel(at, offset, skip, n_kv, n_out, *refs):
    t_ref, q_ref, acc_in, m_in = refs[:4]
    pieces = refs[4 : 4 + n_kv]
    o_refs = refs[4 + n_kv : 4 + n_kv + n_out]
    acc_ref, run_ref, kv_ref, span_ref, sems = refs[4 + n_kv + n_out :]
    fetch(pieces[-1:], [kv_ref], sems)

    def span(step, carry):
        local = t_ref[at.sequence + offset + step]
        stored = t_ref[at.first] + local
        query = rows_of(q_ref, local)
        count = t_ref[at.far_rank + stored]

        @pl.when(count == 0)
        def _():
            acc_ref[...] = acc_in[skip + step]

        for size in range(1, 1 + kv_ref.shape[0]):

            @pl.when(count == size)
            def _(size=size):
                slots = [t_ref[at.far_list + t] - t_ref[at.far_first] for t in range(size)]
                keys, values = gather(kv_ref, slots)
                weights = jnp.exp2(scores(keys, query) - m_in[skip + step, :1])
                acc_ref[...] = acc_in[skip + step] + blend(values, weights)

        recheck(at, t_ref, t_ref[at.order + stored], query, pieces, acc_ref, run_ref, span_ref, sems.at[0])
        for index, o_ref in enumerate(o_refs):

            @pl.when(step == index)
            def _(o_ref=o_ref):
                conclude(acc_ref, o_ref)

        return carry

    lax.fori_loop(0, n_out, span, 0)


def whole_kernel(at, offset, n_kv, count, *refs):
    t_ref, q_ref = refs[:2]
    pieces = refs[2 : 2 + n_kv]
    o_refs = refs[2 + n_kv : -6]
    acc_ref, m_ref, run_ref, kv_ref, span_ref, sems = refs[-6:]
    fetch(pieces, places(at, t_ref, kv_ref, pieces), sems)

    def span(step, carry):
        local = t_ref[at.sequence + offset + step]
        p = t_ref[at.order + t_ref[at.first] + local]
        query = rows_of(q_ref, local)
        attend(t_ref, at.all_list, p, query, kv_ref, acc_ref, m_ref)
        recheck(at, t_ref, p, query, pieces, acc_ref, run_ref, span_ref, sems.at[0])
        if len(o_refs) == 1:
            conclude(acc_ref, rows_of(o_refs[0], local))
        else:
            for index, o_ref in enumerate(o_refs):

                @pl.when(step == index)
                def _(o_ref=o_ref):
                    conclude(acc_ref, o_ref)

        return carry

    lax.fori_loop(0, count, span, 0)


def attention(q, near, far, near_bases, far_bases, far_first, first_span, span_order, sequence):
    q_spans = q.shape[0] // SPAN
    spans = span_order.shape[0]
    at = Table(spans)
    numbers = jnp.arange(spans, dtype=jnp.int32)
    if far:
        is_far = jnp.logical_and(numbers >= far_first, numbers < far_first + far[0].shape[0])
    else:
        is_far = numbers < 0
    head = jnp.stack([first_span, far_first, *near_bases, *far_bases]).astype(jnp.int32)
    head = jnp.pad(head, (0, at.order - head.shape[0]))
    near_lists = listing(span_order, jnp.logical_not(is_far))
    far_lists = listing(span_order, is_far)
    all_list = listing(span_order, numbers >= 0)[1]
    table = jnp.concatenate([head, span_order, *near_lists, *far_lists, all_list, sequence])
    elements = q.shape[0] * GROUP * spans * SPAN // 2
    n_kv = len(near) + len(far)
    smem, vmem = (pl.BlockSpec(memory_space=space) for space in (pltpu.SMEM, pltpu.VMEM))
    acc_like = pltpu.VMEM((HD + EXTRA, ROWS), jnp.float32)
    m_like = pltpu.VMEM((8, ROWS), jnp.float32)
    kv_like = pltpu.VMEM((spans, SPAN + HD, SPAN), jnp.bfloat16)
    span_like = pltpu.VMEM((SPAN + HD, SPAN), jnp.bfloat16)

    def call(kernel, name, operands, pieces, out_shape, scratch_shapes, part):
        return pl.pallas_call(
            kernel,
            in_specs=[smem] + [vmem] * (len(operands) - 1 + len(pieces)),
            out_specs=[vmem] * len(out_shape),
            out_shape=out_shape,
            scratch_shapes=[*scratch_shapes, pltpu.SemaphoreType.DMA((n_kv,))],
            compiler_params=pltpu.CompilerParams(vmem_limit_bytes=VMEM),
            cost_estimate=pl.CostEstimate(
                flops=int(8 * HD * elements * part),
                bytes_accessed=int(4 * q.size * part) + 4 * spans * SPAN * HD,
                transcendentals=int(elements * part),
            ),
            name=name,
        )(*operands, *pieces)

    def begin(offset, count, q):
        shapes = [
            jax.ShapeDtypeStruct((count, HD + EXTRA, ROWS), jnp.float32),
            jax.ShapeDtypeStruct((count, 8, ROWS), jnp.float32),
        ]
        kernel = functools.partial(near_kernel, at, offset, len(near))
        return call(kernel, "near", (table, q), near, shapes, [kv_like], 0.75 * count / q_spans)

    def finish(begun, begun_at, offset, count):
        shapes = [jax.ShapeDtypeStruct((SPAN, GROUP * HD), q.dtype)] * count
        kernel = functools.partial(far_kernel, at, offset, offset - begun_at, n_kv, count)
        scratch = [acc_like, m_like, pltpu.VMEM(far[0].shape, jnp.bfloat16), span_like]
        return call(kernel, "far", (table, q, *begun), near + far, shapes, scratch, 0.25 * count / q_spans)

    def whole(offset, count, q, apart):
        if apart:
            shapes = [jax.ShapeDtypeStruct((SPAN, GROUP * HD), q.dtype)] * count
        else:
            shapes = [jax.ShapeDtypeStruct(q.shape, q.dtype)]
        kernel = functools.partial(whole_kernel, at, offset, n_kv, count)
        scratch = [acc_like, m_like, m_like, kv_like, span_like]
        return call(kernel, "whole", (table, q), near + far, shapes, scratch, count / q_spans)

    return begin, finish, whole


def unpack_kernel(me_ref, *refs):
    parts, (o_ref, sems) = refs[:-2], refs[-2:]
    copies = []
    for index, part in enumerate(parts):
        column = pl.multiple_of((me_ref[0] ^ index) * GROUP * HD, GROUP * HD)
        copies.append(pltpu.make_async_copy(part, o_ref.at[:, pl.ds(column, GROUP * HD)], sems.at[index]))
    for copy in copies:
        copy.start()
    for copy in copies:
        copy.wait()


def to_token_owners(q, begin, finish, whole, me):
    parts = [None] * KVH

    def send(steps, finished):
        for step, done in zip(steps, finished):
            if step:
                done = lax.ppermute(done, GROUP_AXES, [(i, i ^ step) for i in range(KVH)])
            parts[step] = done

    begun = begin(0, sum(map(len, AWAY)), q)
    offset = 0
    for steps in AWAY:
        finished = finish(begun, 0, offset, len(steps))
        send(steps, finished)
        offset += len(steps)
    q, _ = lax.optimization_barrier((q, (finished, [parts[step] for step in AWAY[0]])))
    send(HOME, whole(offset, len(HOME), q, True))
    return pl.pallas_call(
        unpack_kernel,
        in_specs=[pl.BlockSpec(memory_space=pltpu.SMEM)] + [pl.BlockSpec(memory_space=pltpu.VMEM)] * KVH,
        out_specs=pl.BlockSpec(memory_space=pl.ANY),
        out_shape=jax.ShapeDtypeStruct((SPAN, HQ * HD), parts[0].dtype),
        scratch_shapes=[pltpu.SemaphoreType.DMA((KVH,))],
        compiler_params=pltpu.CompilerParams(vmem_limit_bytes=VMEM),
        name="unpack",
    )(me.reshape(1), *parts)


def pack_kernel(k_ref, v_ref, o_ref):
    for h in range(KVH):
        o_ref[h, :SPAN] = k_ref[:, h * HD : (h + 1) * HD]
        o_ref[h, SPAN:] = v_ref[:, h * HD : (h + 1) * HD].T


def to_head_owners(key_rows, value_rows):
    rows = key_rows.shape[0]
    exchange = functools.partial(
        lax.all_to_all, axis_name=GROUP_AXES, split_axis=0, concat_axis=0, tiled=False
    )
    if rows == SPAN:
        packed = pl.pallas_call(
            pack_kernel, out_shape=jax.ShapeDtypeStruct((KVH, SPAN + HD, SPAN), key_rows.dtype), name="pack"
        )(key_rows, value_rows)
        return exchange(packed)
    packed = jnp.concatenate([key_rows.reshape(rows, KVH, HD), value_rows.reshape(rows, KVH, HD)], 2)
    own = exchange(packed.transpose(1, 0, 2)).reshape(KVH * rows // SPAN, SPAN, 2 * HD)
    return jnp.concatenate([own[:, :, :HD], own[:, :, HD:].transpose(0, 2, 1)], 1)


def shards(outer, queries, key_rows, value_rows, span_order):
    rows = queries.shape[0]
    place = lax.axis_index("outer")
    group_rows = KVH * rows
    group_spans = group_rows // SPAN
    own = to_head_owners(key_rows, value_rows)
    q = queries.reshape(rows, KVH, GROUP * HD).transpose(1, 0, 2)
    q = lax.all_to_all(q, GROUP_AXES, split_axis=0, concat_axis=0, tiled=False).reshape(group_rows, GROUP * HD)
    if outer == 4:
        up = lax.ppermute(own, "outer", [(i, (i + 1) % outer) for i in range(outer)])
        down = lax.ppermute(own, "outer", [(i, (i - 1) % outer) for i in range(outer)])
        far = [lax.ppermute(up, "outer", [(i, (i + 1) % outer) for i in range(outer)])]
        near = [own, up, down]
        near_bases = [(place + step) % outer * group_spans for step in (0, outer - 1, 1)]
        far_first = (place + outer - 2) % outer * group_spans
        far_bases = [far_first]
    else:
        near = [lax.all_gather(own, "outer", axis=0, tiled=True)]
        near_bases = [jnp.int32(0)]
        far, far_bases, far_first = [], [], jnp.int32(0)
    me = lax.axis_index(GROUP_AXES).astype(jnp.int32)
    apart = rows == SPAN and outer == 4
    if apart:
        sequence = jnp.stack([me ^ step for steps in (*AWAY, HOME) for step in steps])
    else:
        sequence = jnp.arange(group_spans, dtype=jnp.int32)
    first_span = place * group_spans
    steps = attention(q, near, far, near_bases, far_bases, far_first, first_span, span_order, sequence)
    if apart:
        return to_token_owners(q, *steps, me)
    out = steps[-1](0, group_spans, q, False)[0]
    out = lax.all_to_all(out.reshape(KVH, rows, GROUP * HD), GROUP_AXES, split_axis=0, concat_axis=0, tiled=False)
    return out.transpose(1, 0, 2).reshape(rows, HQ * HD)


def solution(mesh):
    ctx, head = mesh.devices.shape
    inner = KVH // head
    split = Mesh(mesh.devices.reshape(ctx // inner, inner, head), ("outer", "inner", "head"))
    spec = P(("outer", "inner", "head"), None)
    return jax.shard_map(
        functools.partial(shards, ctx // inner),
        mesh=split,
        in_specs=(spec, spec, spec, P()),
        out_specs=spec,
        check_vma=False,
    )
```

```python
import functools
import math

import jax
import jax.numpy as jnp
from jax import lax
from jax.experimental import pallas as pl
from jax.experimental.pallas import tpu as pltpu
from jax.sharding import Mesh
from jax.sharding import PartitionSpec as P

HQ = 64
KVH = 8
HD = 128
SPAN = 128
GROUP = HQ // KVH
ROWS = GROUP * SPAN
SCALE = HD**-0.5 * math.log2(math.e)
EXTRA = 16
BLOCK = 8
VMEM = 24 * 2**20
NT = (((1,), (1,)), ((), ()))
GROUP_AXES = ("inner", "head")
AWAY = ((5, 7), (1, 4, 3, 6))
HOME = (2, 0)


def queries_of(q_ref):
    return jnp.concatenate([q_ref[:, g * HD : (g + 1) * HD] for g in range(GROUP)], 0)


def scores(keys, q_ref):
    return lax.dot_general(keys, queries_of(q_ref), NT, preferred_element_type=jnp.float32) * SCALE


def blend(values, weights):
    ones = jnp.ones((EXTRA, values.shape[1]), jnp.bfloat16)
    values = jnp.concatenate([values, ones], 0)
    return jnp.dot(values, weights.astype(jnp.bfloat16), preferred_element_type=jnp.float32)


def causal(s):
    key = lax.broadcasted_iota(jnp.int32, (SPAN, ROWS), 0)
    row = lax.broadcasted_iota(jnp.int32, (SPAN, ROWS), 1) % SPAN
    return jnp.where(key <= row, s, -1e30)


def gather(kv_ref, slots):
    return (
        jnp.concatenate([kv_ref[s, :SPAN] for s in slots], 0),
        jnp.concatenate([kv_ref[s, SPAN:] for s in slots], 1),
    )


def listing(order, wanted):
    n = order.shape[0]
    numbers = jnp.arange(n, dtype=jnp.int32)
    before = jnp.logical_and(order[None, :] < order[:, None], wanted[None, :])
    rank = jnp.sum(before.astype(jnp.int32), axis=1)
    mine = jnp.logical_and(rank[None, :] == numbers[:, None], wanted[None, :])
    return rank, jnp.sum(jnp.where(mine, numbers[None, :], 0), axis=1)


class Table:
    def __init__(self, spans):
        self.first, self.far_first, self.bases = 0, 1, 2
        self.order = 16
        self.near_rank, self.near_list, self.far_rank, self.far_list, self.all_list = (
            16 + spans * (1 + t) for t in range(5)
        )
        self.sequence = 16 + spans * 6


def fetch(pieces, targets, sems):
    copies = [
        pltpu.make_async_copy(piece, target, sems.at[index])
        for index, (piece, target) in enumerate(zip(pieces, targets))
    ]
    for copy in copies:
        copy.start()
    for copy in copies:
        copy.wait()


def places(at, t_ref, kv_ref, pieces):
    return [kv_ref.at[pl.ds(t_ref[at.bases + i], piece.shape[0])] for i, piece in enumerate(pieces)]


def attend(t_ref, list_at, rank, q_ref, kv_ref, acc_ref, m_ref):
    def first_block(count):
        others = [t_ref[list_at + rank - t] for t in range(1, count)]
        keys, values = gather(kv_ref, [t_ref[list_at + rank], *others])
        s = scores(keys, q_ref)
        own = causal(s[:SPAN])
        m = jnp.max(own, axis=0, keepdims=True)
        s = jnp.concatenate([own, s[SPAN:]], 0) if count > 1 else own
        m_ref[...] = jnp.broadcast_to(m, m_ref.shape)
        acc_ref[...] = blend(values, jnp.exp2(s - m))

    for count in range(1, BLOCK + 1):

        @pl.when(rank % BLOCK == count - 1)
        def _(count=count):
            first_block(count)

    def block(b, carry):
        keys, values = gather(kv_ref, [t_ref[list_at + b * BLOCK + t] for t in range(BLOCK)])
        acc_ref[...] += blend(values, jnp.exp2(scores(keys, q_ref) - m_ref[:1]))
        return carry

    lax.fori_loop(0, rank // BLOCK, block, 0)


def careful(at, t_ref, p, q_ref, pieces, acc_ref, run_ref, span_ref, sem):
    run_ref[...] = jnp.full_like(run_ref, -1e30)
    acc_ref[...] = jnp.zeros_like(acc_ref)
    for index, piece in enumerate(pieces):
        base = t_ref[at.bases + index]

        def visit(j, carry, piece=piece, base=base):
            other = t_ref[at.order + base + j]

            @pl.when(other <= p)
            def _():
                copy = pltpu.make_async_copy(piece.at[j], span_ref, sem)
                copy.start()
                copy.wait()
                s = scores(span_ref[:SPAN], q_ref)
                s = jnp.where(other < p, s, causal(s))
                old = run_ref[...]
                new = jnp.maximum(old, jnp.max(s, axis=0, keepdims=True))
                run_ref[...] = new
                fresh = blend(span_ref[SPAN:], jnp.exp2(s - new[:1]))
                acc_ref[...] = acc_ref[...] * jnp.exp2(old - new)[:1] + fresh

            return carry

        lax.fori_loop(0, piece.shape[0], visit, 0)


def each_span(at, offset, count, t_ref, q_ref, pieces, o_refs, acc_ref, worst_ref, run_ref, span_ref, sem, sums):
    def through(make):
        def span(step, carry):
            local = t_ref[at.sequence + offset + step]
            make(step, local, rows_of(q_ref, local))
            worst_ref[...] = jnp.maximum(worst_ref[...], acc_ref[HD : HD + 8])
            if len(o_refs) == 1:
                conclude(acc_ref, rows_of(o_refs[0], local))
                return carry
            for index, o_ref in enumerate(o_refs):

                @pl.when(step == index)
                def _(o_ref=o_ref):
                    conclude(acc_ref, o_ref)

            return carry

        lax.fori_loop(0, count, span, 0)

    worst_ref[...] = jnp.zeros_like(worst_ref)
    through(sums)

    @pl.when(jnp.logical_not(jnp.max(worst_ref[...]) < 1e30))
    def _():
        def make(step, local, query):
            p = t_ref[at.order + t_ref[at.first] + local]
            careful(at, t_ref, p, query, pieces, acc_ref, run_ref, span_ref, sem)

        through(make)


def conclude(acc_ref, o_ref):
    result = acc_ref[:HD] * (1.0 / acc_ref[HD : HD + 1])
    for g in range(GROUP):
        o_ref[:, g * HD : (g + 1) * HD] = result[:, g * SPAN : (g + 1) * SPAN].T.astype(o_ref.dtype)


def rows_of(ref, span):
    return ref.at[pl.ds(pl.multiple_of(span * SPAN, SPAN), SPAN)]


def near_kernel(at, offset, n_kv, *refs):
    t_ref, q_ref = refs[:2]
    pieces = refs[2 : 2 + n_kv]
    acc_ref, m_ref, kv_ref, sems = refs[2 + n_kv :]
    fetch(pieces, places(at, t_ref, kv_ref, pieces), sems)

    def span(step, carry):
        local = t_ref[at.sequence + offset + step]
        rank = t_ref[at.near_rank + t_ref[at.first] + local]
        attend(t_ref, at.near_list, rank, rows_of(q_ref, local), kv_ref, acc_ref.at[step], m_ref.at[step])
        return carry

    lax.fori_loop(0, acc_ref.shape[0], span, 0)


def far_kernel(at, offset, skip, n_kv, n_out, *refs):
    t_ref, q_ref, acc_in, m_in = refs[:4]
    pieces = refs[4 : 4 + n_kv]
    o_refs = refs[4 + n_kv : 4 + n_kv + n_out]
    kv_ref, acc_ref, worst_ref, run_ref, span_ref, sems = refs[4 + n_kv + n_out :]
    fetch(pieces[-1:], [kv_ref], sems)

    def sums(step, local, query):
        count = t_ref[at.far_rank + t_ref[at.first] + local]

        @pl.when(count == 0)
        def _():
            acc_ref[...] = acc_in[skip + step]

        for size in range(1, 1 + kv_ref.shape[0]):

            @pl.when(count == size)
            def _(size=size):
                slots = [t_ref[at.far_list + t] - t_ref[at.far_first] for t in range(size)]
                keys, values = gather(kv_ref, slots)
                weights = jnp.exp2(scores(keys, query) - m_in[skip + step, :1])
                acc_ref[...] = acc_in[skip + step] + blend(values, weights)

    each_span(
        at, offset, n_out, t_ref, q_ref, pieces, o_refs, acc_ref, worst_ref, run_ref, span_ref, sems.at[0], sums
    )


def whole_kernel(at, offset, n_kv, count, *refs):
    t_ref, q_ref = refs[:2]
    pieces = refs[2 : 2 + n_kv]
    o_refs = refs[2 + n_kv : -7]
    m_ref, kv_ref, acc_ref, worst_ref, run_ref, span_ref, sems = refs[-7:]
    fetch(pieces, places(at, t_ref, kv_ref, pieces), sems)

    def sums(step, local, query):
        p = t_ref[at.order + t_ref[at.first] + local]
        attend(t_ref, at.all_list, p, query, kv_ref, acc_ref, m_ref)

    each_span(
        at, offset, count, t_ref, q_ref, pieces, o_refs, acc_ref, worst_ref, run_ref, span_ref, sems.at[0], sums
    )


def attention(q, near, far, near_bases, far_bases, far_first, first_span, span_order, sequence):
    q_spans = q.shape[0] // SPAN
    spans = span_order.shape[0]
    at = Table(spans)
    numbers = jnp.arange(spans, dtype=jnp.int32)
    if far:
        is_far = jnp.logical_and(numbers >= far_first, numbers < far_first + far[0].shape[0])
    else:
        is_far = numbers < 0
    head = jnp.stack([first_span, far_first, *near_bases, *far_bases]).astype(jnp.int32)
    head = jnp.pad(head, (0, at.order - head.shape[0]))
    near_lists = listing(span_order, jnp.logical_not(is_far))
    far_lists = listing(span_order, is_far)
    all_list = listing(span_order, numbers >= 0)[1]
    table = jnp.concatenate([head, span_order, *near_lists, *far_lists, all_list, sequence])
    elements = q.shape[0] * GROUP * spans * SPAN // 2
    n_kv = len(near) + len(far)
    smem, vmem = (pl.BlockSpec(memory_space=space) for space in (pltpu.SMEM, pltpu.VMEM))
    acc_like = pltpu.VMEM((HD + EXTRA, ROWS), jnp.float32)
    m_like = pltpu.VMEM((8, ROWS), jnp.float32)
    kv_like = pltpu.VMEM((spans, SPAN + HD, SPAN), jnp.bfloat16)
    span_like = pltpu.VMEM((SPAN + HD, SPAN), jnp.bfloat16)

    def call(kernel, name, operands, pieces, out_shape, scratch_shapes, part):
        return pl.pallas_call(
            kernel,
            in_specs=[smem] + [vmem] * (len(operands) - 1 + len(pieces)),
            out_specs=[vmem] * len(out_shape),
            out_shape=out_shape,
            scratch_shapes=[*scratch_shapes, pltpu.SemaphoreType.DMA((n_kv,))],
            compiler_params=pltpu.CompilerParams(vmem_limit_bytes=VMEM),
            cost_estimate=pl.CostEstimate(
                flops=int(8 * HD * elements * part),
                bytes_accessed=int(4 * q.size * part) + 4 * spans * SPAN * HD,
                transcendentals=int(elements * part),
            ),
            name=name,
        )(*operands, *pieces)

    def begin(offset, count, q):
        shapes = [
            jax.ShapeDtypeStruct((count, HD + EXTRA, ROWS), jnp.float32),
            jax.ShapeDtypeStruct((count, 8, ROWS), jnp.float32),
        ]
        kernel = functools.partial(near_kernel, at, offset, len(near))
        return call(kernel, "near", (table, q), near, shapes, [kv_like], 0.75 * count / q_spans)

    def finish(begun, begun_at, offset, count):
        shapes = [jax.ShapeDtypeStruct((SPAN, GROUP * HD), q.dtype)] * count
        kernel = functools.partial(far_kernel, at, offset, offset - begun_at, n_kv, count)
        scratch = [pltpu.VMEM(far[0].shape, jnp.bfloat16), acc_like, m_like, m_like, span_like]
        return call(kernel, "far", (table, q, *begun), near + far, shapes, scratch, 0.25 * count / q_spans)

    def whole(offset, count, q, apart):
        if apart:
            shapes = [jax.ShapeDtypeStruct((SPAN, GROUP * HD), q.dtype)] * count
        else:
            shapes = [jax.ShapeDtypeStruct(q.shape, q.dtype)]
        kernel = functools.partial(whole_kernel, at, offset, n_kv, count)
        scratch = [m_like, kv_like, acc_like, m_like, m_like, span_like]
        return call(kernel, "whole", (table, q), near + far, shapes, scratch, count / q_spans)

    return begin, finish, whole


def unpack_kernel(me_ref, *refs):
    parts, (o_ref, sems) = refs[:-2], refs[-2:]
    copies = []
    for index, part in enumerate(parts):
        column = pl.multiple_of((me_ref[0] ^ index) * GROUP * HD, GROUP * HD)
        copies.append(pltpu.make_async_copy(part, o_ref.at[:, pl.ds(column, GROUP * HD)], sems.at[index]))
    for copy in copies:
        copy.start()
    for copy in copies:
        copy.wait()


def to_token_owners(q, begin, finish, whole, me):
    parts = [None] * KVH

    def send(steps, finished):
        for step, done in zip(steps, finished):
            if step:
                done = lax.ppermute(done, GROUP_AXES, [(i, i ^ step) for i in range(KVH)])
            parts[step] = done

    begun = begin(0, sum(map(len, AWAY)), q)
    offset = 0
    for steps in AWAY:
        finished = finish(begun, 0, offset, len(steps))
        send(steps, finished)
        offset += len(steps)
    q, _ = lax.optimization_barrier((q, (finished, [parts[step] for step in AWAY[0]])))
    send(HOME, whole(offset, len(HOME), q, True))
    return pl.pallas_call(
        unpack_kernel,
        in_specs=[pl.BlockSpec(memory_space=pltpu.SMEM)] + [pl.BlockSpec(memory_space=pltpu.VMEM)] * KVH,
        out_specs=pl.BlockSpec(memory_space=pl.ANY),
        out_shape=jax.ShapeDtypeStruct((SPAN, HQ * HD), parts[0].dtype),
        scratch_shapes=[pltpu.SemaphoreType.DMA((KVH,))],
        compiler_params=pltpu.CompilerParams(vmem_limit_bytes=VMEM),
        name="unpack",
    )(me.reshape(1), *parts)


def pack_kernel(k_ref, v_ref, o_ref):
    for h in range(KVH):
        o_ref[h, :SPAN] = k_ref[:, h * HD : (h + 1) * HD]
        o_ref[h, SPAN:] = v_ref[:, h * HD : (h + 1) * HD].T


def to_head_owners(key_rows, value_rows):
    rows = key_rows.shape[0]
    exchange = functools.partial(
        lax.all_to_all, axis_name=GROUP_AXES, split_axis=0, concat_axis=0, tiled=False
    )
    if rows == SPAN:
        packed = pl.pallas_call(
            pack_kernel, out_shape=jax.ShapeDtypeStruct((KVH, SPAN + HD, SPAN), key_rows.dtype), name="pack"
        )(key_rows, value_rows)
        return exchange(packed)
    packed = jnp.concatenate([key_rows.reshape(rows, KVH, HD), value_rows.reshape(rows, KVH, HD)], 2)
    own = exchange(packed.transpose(1, 0, 2)).reshape(KVH * rows // SPAN, SPAN, 2 * HD)
    return jnp.concatenate([own[:, :, :HD], own[:, :, HD:].transpose(0, 2, 1)], 1)


def shards(outer, queries, key_rows, value_rows, span_order):
    rows = queries.shape[0]
    place = lax.axis_index("outer")
    group_rows = KVH * rows
    group_spans = group_rows // SPAN
    own = to_head_owners(key_rows, value_rows)
    q = queries.reshape(rows, KVH, GROUP * HD).transpose(1, 0, 2)
    q = lax.all_to_all(q, GROUP_AXES, split_axis=0, concat_axis=0, tiled=False).reshape(group_rows, GROUP * HD)
    if outer == 4:
        up = lax.ppermute(own, "outer", [(i, (i + 1) % outer) for i in range(outer)])
        down = lax.ppermute(own, "outer", [(i, (i - 1) % outer) for i in range(outer)])
        far = [lax.ppermute(up, "outer", [(i, (i + 1) % outer) for i in range(outer)])]
        near = [own, up, down]
        near_bases = [(place + step) % outer * group_spans for step in (0, outer - 1, 1)]
        far_first = (place + outer - 2) % outer * group_spans
        far_bases = [far_first]
    else:
        near = [lax.all_gather(own, "outer", axis=0, tiled=True)]
        near_bases = [jnp.int32(0)]
        far, far_bases, far_first = [], [], jnp.int32(0)
    me = lax.axis_index(GROUP_AXES).astype(jnp.int32)
    apart = rows == SPAN and outer == 4
    if apart:
        sequence = jnp.stack([me ^ step for steps in (*AWAY, HOME) for step in steps])
    else:
        sequence = jnp.arange(group_spans, dtype=jnp.int32)
    first_span = place * group_spans
    steps = attention(q, near, far, near_bases, far_bases, far_first, first_span, span_order, sequence)
    if apart:
        return to_token_owners(q, *steps, me)
    out = steps[-1](0, group_spans, q, False)[0]
    out = lax.all_to_all(out.reshape(KVH, rows, GROUP * HD), GROUP_AXES, split_axis=0, concat_axis=0, tiled=False)
    return out.transpose(1, 0, 2).reshape(rows, HQ * HD)


def solution(mesh):
    ctx, head = mesh.devices.shape
    inner = KVH // head
    split = Mesh(mesh.devices.reshape(ctx // inner, inner, head), ("outer", "inner", "head"))
    spec = P(("outer", "inner", "head"), None)
    return jax.shard_map(
        functools.partial(shards, ctx // inner),
        mesh=split,
        in_specs=(spec, spec, spec, P()),
        out_specs=spec,
        check_vma=False,
    )
```

```python
import functools
import math

import jax
import jax.numpy as jnp
from jax import lax
from jax.experimental import pallas as pl
from jax.experimental.pallas import tpu as pltpu
from jax.sharding import Mesh
from jax.sharding import PartitionSpec as P

HQ = 64
KVH = 8
HD = 128
SPAN = 128
GROUP = HQ // KVH
ROWS = GROUP * SPAN
SCALE = HD**-0.5 * math.log2(math.e)
EXTRA = 16
BLOCK = 8
VMEM = 24 * 2**20
NT = (((1,), (1,)), ((), ()))
GROUP_AXES = ("inner", "head")
AWAY = ((5, 7), (1, 4, 3, 6))
HOME = (2, 0)


def queries_of(q_ref):
    return jnp.concatenate([q_ref[:, g * HD : (g + 1) * HD] for g in range(GROUP)], 0)


def scores(keys, q_ref):
    return lax.dot_general(keys, queries_of(q_ref), NT, preferred_element_type=jnp.float32) * SCALE


def blend(values, weights):
    ones = jnp.ones((EXTRA, values.shape[1]), jnp.bfloat16)
    values = jnp.concatenate([values, ones], 0)
    return jnp.dot(values, weights.astype(jnp.bfloat16), preferred_element_type=jnp.float32)


def causal(s):
    key = lax.broadcasted_iota(jnp.int32, (SPAN, ROWS), 0)
    row = lax.broadcasted_iota(jnp.int32, (SPAN, ROWS), 1) % SPAN
    return jnp.where(key <= row, s, -1e30)


def gather(kv_ref, slots):
    return (
        jnp.concatenate([kv_ref[s, :SPAN] for s in slots], 0),
        jnp.concatenate([kv_ref[s, SPAN:] for s in slots], 1),
    )


def listing(order, wanted):
    n = order.shape[0]
    numbers = jnp.arange(n, dtype=jnp.int32)
    before = jnp.logical_and(order[None, :] < order[:, None], wanted[None, :])
    rank = jnp.sum(before.astype(jnp.int32), axis=1)
    mine = jnp.logical_and(rank[None, :] == numbers[:, None], wanted[None, :])
    return rank, jnp.sum(jnp.where(mine, numbers[None, :], 0), axis=1)


class Table:
    def __init__(self, spans):
        self.first, self.far_first, self.bases = 0, 1, 2
        self.order = 16
        self.near_rank, self.near_list, self.far_rank, self.far_list, self.all_list = (
            16 + spans * (1 + t) for t in range(5)
        )
        self.sequence = 16 + spans * 6


def fetch(pieces, targets, sems):
    copies = [
        pltpu.make_async_copy(piece, target, sems.at[index])
        for index, (piece, target) in enumerate(zip(pieces, targets))
    ]
    for copy in copies:
        copy.start()
    for copy in copies:
        copy.wait()


def places(at, t_ref, kv_ref, pieces):
    return [kv_ref.at[pl.ds(t_ref[at.bases + i], piece.shape[0])] for i, piece in enumerate(pieces)]


def attend(t_ref, list_at, rank, q_ref, kv_ref, acc_ref, m_ref):
    def first_block(count):
        others = [t_ref[list_at + rank - t] for t in range(1, count)]
        keys, values = gather(kv_ref, [t_ref[list_at + rank], *others])
        s = scores(keys, q_ref)
        own = causal(s[:SPAN])
        m = jnp.max(own, axis=0, keepdims=True)
        s = jnp.concatenate([own, s[SPAN:]], 0) if count > 1 else own
        m_ref[...] = jnp.broadcast_to(m, m_ref.shape)
        acc_ref[...] = blend(values, jnp.exp2(s - m))

    for count in range(1, BLOCK + 1):

        @pl.when(rank % BLOCK == count - 1)
        def _(count=count):
            first_block(count)

    def block(b, carry):
        keys, values = gather(kv_ref, [t_ref[list_at + b * BLOCK + t] for t in range(BLOCK)])
        acc_ref[...] += blend(values, jnp.exp2(scores(keys, q_ref) - m_ref[:1]))
        return carry

    lax.fori_loop(0, rank // BLOCK, block, 0)


def careful(at, t_ref, p, q_ref, pieces, acc_ref, run_ref, span_ref, sem):
    run_ref[...] = jnp.full_like(run_ref, -1e30)
    acc_ref[...] = jnp.zeros_like(acc_ref)
    for index, piece in enumerate(pieces):
        base = t_ref[at.bases + index]

        def visit(j, carry, piece=piece, base=base):
            other = t_ref[at.order + base + j]

            @pl.when(other <= p)
            def _():
                copy = pltpu.make_async_copy(piece.at[j], span_ref, sem)
                copy.start()
                copy.wait()
                s = scores(span_ref[:SPAN], q_ref)
                s = jnp.where(other < p, s, causal(s))
                old = run_ref[...]
                new = jnp.maximum(old, jnp.max(s, axis=0, keepdims=True))
                run_ref[...] = new
                fresh = blend(span_ref[SPAN:], jnp.exp2(s - new[:1]))
                acc_ref[...] = acc_ref[...] * jnp.exp2(old - new)[:1] + fresh

            return carry

        lax.fori_loop(0, piece.shape[0], visit, 0)


def each_span(at, offset, count, t_ref, q_ref, pieces, o_refs, acc_ref, worst_ref, run_ref, span_ref, sem, sums):
    def through(make):
        def span(step, carry):
            local = t_ref[at.sequence + offset + step]
            make(step, local, rows_of(q_ref, local))
            worst_ref[...] = jnp.maximum(worst_ref[...], acc_ref[HD : HD + 8])
            if len(o_refs) == 1:
                conclude(acc_ref, rows_of(o_refs[0], local))
                return carry
            for index, o_ref in enumerate(o_refs):

                @pl.when(step == index)
                def _(o_ref=o_ref):
                    conclude(acc_ref, o_ref)

            return carry

        lax.fori_loop(0, count, span, 0)

    worst_ref[...] = jnp.zeros_like(worst_ref)
    through(sums)

    @pl.when(jnp.logical_not(jnp.max(worst_ref[...]) < 1e30))
    def _():
        def make(step, local, query):
            p = t_ref[at.order + t_ref[at.first] + local]
            careful(at, t_ref, p, query, pieces, acc_ref, run_ref, span_ref, sem)

        through(make)


def conclude(acc_ref, o_ref):
    result = acc_ref[:HD] * (1.0 / acc_ref[HD : HD + 1])
    for g in range(GROUP):
        o_ref[:, g * HD : (g + 1) * HD] = result[:, g * SPAN : (g + 1) * SPAN].T.astype(o_ref.dtype)


def rows_of(ref, span):
    return ref.at[pl.ds(pl.multiple_of(span * SPAN, SPAN), SPAN)]


def near_kernel(at, offset, n_kv, *refs):
    t_ref, q_ref = refs[:2]
    pieces = refs[2 : 2 + n_kv]
    acc_ref, m_ref, kv_ref, sems = refs[2 + n_kv :]
    fetch(pieces, places(at, t_ref, kv_ref, pieces), sems)

    def span(step, carry):
        local = t_ref[at.sequence + offset + step]
        rank = t_ref[at.near_rank + t_ref[at.first] + local]
        attend(t_ref, at.near_list, rank, rows_of(q_ref, local), kv_ref, acc_ref.at[step], m_ref.at[step])
        return carry

    lax.fori_loop(0, acc_ref.shape[0], span, 0)


def far_kernel(at, offset, skip, n_kv, n_out, *refs):
    t_ref, q_ref, acc_in, m_in = refs[:4]
    pieces = refs[4 : 4 + n_kv]
    o_refs = refs[4 + n_kv : 4 + n_kv + n_out]
    acc_ref, worst_ref, run_ref, span_ref, sems = refs[4 + n_kv + n_out :]
    kv_ref = pieces[-1]

    def sums(step, local, query):
        count = t_ref[at.far_rank + t_ref[at.first] + local]

        @pl.when(count == 0)
        def _():
            acc_ref[...] = acc_in[skip + step]

        for size in range(1, 1 + kv_ref.shape[0]):

            @pl.when(count == size)
            def _(size=size):
                slots = [t_ref[at.far_list + t] - t_ref[at.far_first] for t in range(size)]
                keys, values = gather(kv_ref, slots)
                weights = jnp.exp2(scores(keys, query) - m_in[skip + step, :1])
                acc_ref[...] = acc_in[skip + step] + blend(values, weights)

    each_span(
        at, offset, n_out, t_ref, q_ref, pieces, o_refs, acc_ref, worst_ref, run_ref, span_ref, sems.at[0], sums
    )


def whole_kernel(at, offset, n_kv, count, *refs):
    t_ref, q_ref = refs[:2]
    pieces = refs[2 : 2 + n_kv]
    o_refs = refs[2 + n_kv : -7]
    m_ref, kv_ref, acc_ref, worst_ref, run_ref, span_ref, sems = refs[-7:]
    fetch(pieces, places(at, t_ref, kv_ref, pieces), sems)

    def sums(step, local, query):
        p = t_ref[at.order + t_ref[at.first] + local]
        attend(t_ref, at.all_list, p, query, kv_ref, acc_ref, m_ref)

    each_span(
        at, offset, count, t_ref, q_ref, pieces, o_refs, acc_ref, worst_ref, run_ref, span_ref, sems.at[0], sums
    )


def attention(q, near, far, near_bases, far_bases, far_first, first_span, span_order, sequence):
    q_spans = q.shape[0] // SPAN
    spans = span_order.shape[0]
    at = Table(spans)
    numbers = jnp.arange(spans, dtype=jnp.int32)
    if far:
        is_far = jnp.logical_and(numbers >= far_first, numbers < far_first + far[0].shape[0])
    else:
        is_far = numbers < 0
    head = jnp.stack([first_span, far_first, *near_bases, *far_bases]).astype(jnp.int32)
    head = jnp.pad(head, (0, at.order - head.shape[0]))
    near_lists = listing(span_order, jnp.logical_not(is_far))
    far_lists = listing(span_order, is_far)
    all_list = listing(span_order, numbers >= 0)[1]
    table = jnp.concatenate([head, span_order, *near_lists, *far_lists, all_list, sequence])
    elements = q.shape[0] * GROUP * spans * SPAN // 2
    n_kv = len(near) + len(far)
    smem, vmem, anywhere = (pl.BlockSpec(memory_space=space) for space in (pltpu.SMEM, pltpu.VMEM, pl.ANY))
    acc_like = pltpu.VMEM((HD + EXTRA, ROWS), jnp.float32)
    m_like = pltpu.VMEM((8, ROWS), jnp.float32)
    kv_like = pltpu.VMEM((spans, SPAN + HD, SPAN), jnp.bfloat16)
    span_like = pltpu.VMEM((SPAN + HD, SPAN), jnp.bfloat16)

    def call(kernel, name, operands, pieces, out_shape, scratch_shapes, part, in_place=0):
        spaces = [anywhere] * (len(pieces) - in_place) + [vmem] * in_place
        return pl.pallas_call(
            kernel,
            in_specs=[smem] + [vmem] * (len(operands) - 1) + spaces,
            out_specs=[vmem] * len(out_shape),
            out_shape=out_shape,
            scratch_shapes=[*scratch_shapes, pltpu.SemaphoreType.DMA((n_kv,))],
            compiler_params=pltpu.CompilerParams(vmem_limit_bytes=VMEM),
            cost_estimate=pl.CostEstimate(
                flops=int(8 * HD * elements * part),
                bytes_accessed=int(4 * q.size * part) + 4 * spans * SPAN * HD,
                transcendentals=int(elements * part),
            ),
            name=name,
        )(*operands, *pieces)

    def begin(offset, count, q):
        shapes = [
            jax.ShapeDtypeStruct((count, HD + EXTRA, ROWS), jnp.float32),
            jax.ShapeDtypeStruct((count, 8, ROWS), jnp.float32),
        ]
        kernel = functools.partial(near_kernel, at, offset, len(near))
        return call(kernel, "near", (table, q), near, shapes, [kv_like], 0.75 * count / q_spans)

    def finish(begun, begun_at, offset, count):
        shapes = [jax.ShapeDtypeStruct((SPAN, GROUP * HD), q.dtype)] * count
        kernel = functools.partial(far_kernel, at, offset, offset - begun_at, n_kv, count)
        scratch = [acc_like, m_like, m_like, span_like]
        return call(kernel, "far", (table, q, *begun), near + far, shapes, scratch, 0.25 * count / q_spans, 1)

    def whole(offset, count, q, apart):
        if apart:
            shapes = [jax.ShapeDtypeStruct((SPAN, GROUP * HD), q.dtype)] * count
        else:
            shapes = [jax.ShapeDtypeStruct(q.shape, q.dtype)]
        kernel = functools.partial(whole_kernel, at, offset, n_kv, count)
        scratch = [m_like, kv_like, acc_like, m_like, m_like, span_like]
        return call(kernel, "whole", (table, q), near + far, shapes, scratch, count / q_spans)

    return begin, finish, whole


def unpack_kernel(me_ref, *refs):
    parts, (o_ref, sems) = refs[:-2], refs[-2:]
    copies = []
    for index, part in enumerate(parts):
        column = pl.multiple_of((me_ref[0] ^ index) * GROUP * HD, GROUP * HD)
        copies.append(pltpu.make_async_copy(part, o_ref.at[:, pl.ds(column, GROUP * HD)], sems.at[index]))
    for copy in copies:
        copy.start()
    for copy in copies:
        copy.wait()


def to_token_owners(q, begin, finish, whole, me):
    parts = [None] * KVH

    def send(steps, finished):
        for step, done in zip(steps, finished):
            if step:
                done = lax.ppermute(done, GROUP_AXES, [(i, i ^ step) for i in range(KVH)])
            parts[step] = done

    begun = begin(0, sum(map(len, AWAY)), q)
    offset = 0
    for steps in AWAY:
        finished = finish(begun, 0, offset, len(steps))
        send(steps, finished)
        offset += len(steps)
    q, _ = lax.optimization_barrier((q, (finished, [parts[step] for step in AWAY[0]])))
    send(HOME, whole(offset, len(HOME), q, True))
    return pl.pallas_call(
        unpack_kernel,
        in_specs=[pl.BlockSpec(memory_space=pltpu.SMEM)] + [pl.BlockSpec(memory_space=pltpu.VMEM)] * KVH,
        out_specs=pl.BlockSpec(memory_space=pl.ANY),
        out_shape=jax.ShapeDtypeStruct((SPAN, HQ * HD), parts[0].dtype),
        scratch_shapes=[pltpu.SemaphoreType.DMA((KVH,))],
        compiler_params=pltpu.CompilerParams(vmem_limit_bytes=VMEM),
        name="unpack",
    )(me.reshape(1), *parts)


def pack_kernel(k_ref, v_ref, o_ref):
    for h in range(KVH):
        o_ref[h, :SPAN] = k_ref[:, h * HD : (h + 1) * HD]
        o_ref[h, SPAN:] = v_ref[:, h * HD : (h + 1) * HD].T


def to_head_owners(key_rows, value_rows):
    rows = key_rows.shape[0]
    exchange = functools.partial(
        lax.all_to_all, axis_name=GROUP_AXES, split_axis=0, concat_axis=0, tiled=False
    )
    if rows == SPAN:
        packed = pl.pallas_call(
            pack_kernel, out_shape=jax.ShapeDtypeStruct((KVH, SPAN + HD, SPAN), key_rows.dtype), name="pack"
        )(key_rows, value_rows)
        return exchange(packed)
    packed = jnp.concatenate([key_rows.reshape(rows, KVH, HD), value_rows.reshape(rows, KVH, HD)], 2)
    own = exchange(packed.transpose(1, 0, 2)).reshape(KVH * rows // SPAN, SPAN, 2 * HD)
    return jnp.concatenate([own[:, :, :HD], own[:, :, HD:].transpose(0, 2, 1)], 1)


def shards(outer, queries, key_rows, value_rows, span_order):
    rows = queries.shape[0]
    place = lax.axis_index("outer")
    group_rows = KVH * rows
    group_spans = group_rows // SPAN
    own = to_head_owners(key_rows, value_rows)
    q = queries.reshape(rows, KVH, GROUP * HD).transpose(1, 0, 2)
    q = lax.all_to_all(q, GROUP_AXES, split_axis=0, concat_axis=0, tiled=False).reshape(group_rows, GROUP * HD)
    if outer == 4:
        up = lax.ppermute(own, "outer", [(i, (i + 1) % outer) for i in range(outer)])
        down = lax.ppermute(own, "outer", [(i, (i - 1) % outer) for i in range(outer)])
        far = [lax.ppermute(up, "outer", [(i, (i + 1) % outer) for i in range(outer)])]
        near = [own, up, down]
        near_bases = [(place + step) % outer * group_spans for step in (0, outer - 1, 1)]
        far_first = (place + outer - 2) % outer * group_spans
        far_bases = [far_first]
    else:
        near = [lax.all_gather(own, "outer", axis=0, tiled=True)]
        near_bases = [jnp.int32(0)]
        far, far_bases, far_first = [], [], jnp.int32(0)
    me = lax.axis_index(GROUP_AXES).astype(jnp.int32)
    apart = rows == SPAN and outer == 4
    if apart:
        sequence = jnp.stack([me ^ step for steps in (*AWAY, HOME) for step in steps])
    else:
        sequence = jnp.arange(group_spans, dtype=jnp.int32)
    first_span = place * group_spans
    steps = attention(q, near, far, near_bases, far_bases, far_first, first_span, span_order, sequence)
    if apart:
        return to_token_owners(q, *steps, me)
    out = steps[-1](0, group_spans, q, False)[0]
    out = lax.all_to_all(out.reshape(KVH, rows, GROUP * HD), GROUP_AXES, split_axis=0, concat_axis=0, tiled=False)
    return out.transpose(1, 0, 2).reshape(rows, HQ * HD)


def solution(mesh):
    ctx, head = mesh.devices.shape
    inner = KVH // head
    split = Mesh(mesh.devices.reshape(ctx // inner, inner, head), ("outer", "inner", "head"))
    spec = P(("outer", "inner", "head"), None)
    return jax.shard_map(
        functools.partial(shards, ctx // inner),
        mesh=split,
        in_specs=(spec, spec, spec, P()),
        out_specs=spec,
        check_vma=False,
    )
```

```python
import functools
import math

import jax
import jax.numpy as jnp
from jax import lax
from jax.experimental import pallas as pl
from jax.experimental.pallas import tpu as pltpu
from jax.sharding import Mesh
from jax.sharding import PartitionSpec as P

HQ = 64
KVH = 8
HD = 128
SPAN = 128
GROUP = HQ // KVH
ROWS = GROUP * SPAN
SCALE = HD**-0.5 * math.log2(math.e)
EXTRA = 16
BLOCK = 8
VMEM = 24 * 2**20
NT = (((1,), (1,)), ((), ()))
GROUP_AXES = ("inner", "head")
AWAY = ((5, 7), (1, 4, 3, 6))
HOME = (2, 0)


def queries_of(q_ref):
    return jnp.concatenate([q_ref[:, g * HD : (g + 1) * HD] for g in range(GROUP)], 0)


def scores(keys, q_ref):
    return lax.dot_general(keys, queries_of(q_ref), NT, preferred_element_type=jnp.float32) * SCALE


def blend(values, weights):
    ones = jnp.ones((EXTRA, values.shape[1]), jnp.bfloat16)
    values = jnp.concatenate([values, ones], 0)
    return jnp.dot(values, weights.astype(jnp.bfloat16), preferred_element_type=jnp.float32)


def causal(s):
    key = lax.broadcasted_iota(jnp.int32, (SPAN, ROWS), 0)
    row = lax.broadcasted_iota(jnp.int32, (SPAN, ROWS), 1) % SPAN
    return jnp.where(key <= row, s, -1e30)


def gather(kv_ref, slots):
    return (
        jnp.concatenate([kv_ref[s, :SPAN] for s in slots], 0),
        jnp.concatenate([kv_ref[s, SPAN:] for s in slots], 1),
    )


def listing(order, wanted):
    n = order.shape[0]
    numbers = jnp.arange(n, dtype=jnp.int32)
    before = jnp.logical_and(order[None, :] < order[:, None], wanted[None, :])
    rank = jnp.sum(before.astype(jnp.int32), axis=1)
    mine = jnp.logical_and(rank[None, :] == numbers[:, None], wanted[None, :])
    return rank, jnp.sum(jnp.where(mine, numbers[None, :], 0), axis=1)


class Table:
    def __init__(self, spans):
        self.first, self.far_first, self.bases = 0, 1, 2
        self.order = 16
        self.near_rank, self.near_list, self.far_rank, self.far_list, self.all_list = (
            16 + spans * (1 + t) for t in range(5)
        )
        self.sequence = 16 + spans * 6


def fetch(pieces, targets, sems):
    copies = [
        pltpu.make_async_copy(piece, target, sems.at[index])
        for index, (piece, target) in enumerate(zip(pieces, targets))
    ]
    for copy in copies:
        copy.start()
    for copy in copies:
        copy.wait()


def places(at, t_ref, kv_ref, pieces):
    return [kv_ref.at[pl.ds(t_ref[at.bases + i], piece.shape[0])] for i, piece in enumerate(pieces)]


def attend(t_ref, list_at, rank, q_ref, kv_ref, acc_ref, m_ref):
    def first_block(count):
        others = [t_ref[list_at + rank - t] for t in range(1, count)]
        keys, values = gather(kv_ref, [t_ref[list_at + rank], *others])
        s = scores(keys, q_ref)
        own = causal(s[:SPAN])
        m = jnp.max(own, axis=0, keepdims=True)
        s = jnp.concatenate([own, s[SPAN:]], 0) if count > 1 else own
        m_ref[...] = jnp.broadcast_to(m, m_ref.shape)
        acc_ref[...] = blend(values, jnp.exp2(s - m))

    for count in range(1, BLOCK + 1):

        @pl.when(rank % BLOCK == count - 1)
        def _(count=count):
            first_block(count)

    def block(b, carry):
        keys, values = gather(kv_ref, [t_ref[list_at + b * BLOCK + t] for t in range(BLOCK)])
        acc_ref[...] += blend(values, jnp.exp2(scores(keys, q_ref) - m_ref[:1]))
        return carry

    lax.fori_loop(0, rank // BLOCK, block, 0)


def careful(at, t_ref, p, q_ref, pieces, acc_ref, run_ref, span_ref, sem):
    run_ref[...] = jnp.full_like(run_ref, -1e30)
    acc_ref[...] = jnp.zeros_like(acc_ref)
    for index, piece in enumerate(pieces):
        base = t_ref[at.bases + index]

        def visit(j, carry, piece=piece, base=base):
            other = t_ref[at.order + base + j]

            @pl.when(other <= p)
            def _():
                copy = pltpu.make_async_copy(piece.at[j], span_ref, sem)
                copy.start()
                copy.wait()
                s = scores(span_ref[:SPAN], q_ref)
                s = jnp.where(other < p, s, causal(s))
                old = run_ref[...]
                new = jnp.maximum(old, jnp.max(s, axis=0, keepdims=True))
                run_ref[...] = new
                fresh = blend(span_ref[SPAN:], jnp.exp2(s - new[:1]))
                acc_ref[...] = acc_ref[...] * jnp.exp2(old - new)[:1] + fresh

            return carry

        lax.fori_loop(0, piece.shape[0], visit, 0)


def each_span(at, offset, count, t_ref, q_ref, pieces, o_refs, acc_ref, worst_ref, run_ref, span_ref, sem, sums):
    def through(make):
        def span(step, carry):
            local = t_ref[at.sequence + offset + step]
            make(step, local, rows_of(q_ref, local))
            worst_ref[...] = jnp.maximum(worst_ref[...], acc_ref[HD : HD + 8])
            if len(o_refs) == 1:
                conclude(acc_ref, rows_of(o_refs[0], local))
                return carry
            for index, o_ref in enumerate(o_refs):

                @pl.when(step == index)
                def _(o_ref=o_ref):
                    conclude(acc_ref, o_ref)

            return carry

        lax.fori_loop(0, count, span, 0)

    worst_ref[...] = jnp.zeros_like(worst_ref)
    through(sums)

    @pl.when(jnp.logical_not(jnp.max(worst_ref[...]) < 1e30))
    def _():
        def make(step, local, query):
            p = t_ref[at.order + t_ref[at.first] + local]
            careful(at, t_ref, p, query, pieces, acc_ref, run_ref, span_ref, sem)

        through(make)


def conclude(acc_ref, o_ref):
    result = acc_ref[:HD] * (1.0 / acc_ref[HD : HD + 1])
    for g in range(GROUP):
        o_ref[:, g * HD : (g + 1) * HD] = result[:, g * SPAN : (g + 1) * SPAN].T.astype(o_ref.dtype)


def rows_of(ref, span):
    return ref.at[pl.ds(pl.multiple_of(span * SPAN, SPAN), SPAN)]


def near_kernel(at, offset, n_kv, *refs):
    t_ref, q_ref = refs[:2]
    pieces = refs[2 : 2 + n_kv]
    acc_ref, m_ref, kv_ref, sems = refs[2 + n_kv :]
    fetch(pieces, places(at, t_ref, kv_ref, pieces), sems)

    def span(step, carry):
        local = t_ref[at.sequence + offset + step]
        rank = t_ref[at.near_rank + t_ref[at.first] + local]
        attend(t_ref, at.near_list, rank, rows_of(q_ref, local), kv_ref, acc_ref.at[step], m_ref.at[step])
        return carry

    lax.fori_loop(0, acc_ref.shape[0], span, 0)


def far_kernel(at, offset, skip, n_kv, n_out, *refs):
    t_ref, q_ref, acc_in, m_in = refs[:4]
    pieces = refs[4 : 4 + n_kv]
    o_refs = refs[4 + n_kv : 4 + n_kv + n_out]
    acc_ref, worst_ref, run_ref, span_ref, sems = refs[4 + n_kv + n_out :]
    kv_ref = pieces[-1]

    def sums(step, local, query):
        count = t_ref[at.far_rank + t_ref[at.first] + local]

        @pl.when(count == 0)
        def _():
            acc_ref[...] = acc_in[skip + step]

        for size in range(1, 1 + kv_ref.shape[0]):

            @pl.when(count == size)
            def _(size=size):
                slots = [t_ref[at.far_list + t] - t_ref[at.far_first] for t in range(size)]
                keys, values = gather(kv_ref, slots)
                weights = jnp.exp2(scores(keys, query) - m_in[skip + step, :1])
                acc_ref[...] = acc_in[skip + step] + blend(values, weights)

    each_span(
        at, offset, n_out, t_ref, q_ref, pieces, o_refs, acc_ref, worst_ref, run_ref, span_ref, sems.at[0], sums
    )


def whole_kernel(at, offset, n_kv, count, *refs):
    t_ref, q_ref = refs[:2]
    pieces = refs[2 : 2 + n_kv]
    o_refs = refs[2 + n_kv : -7]
    m_ref, kv_ref, acc_ref, worst_ref, run_ref, span_ref, sems = refs[-7:]
    fetch(pieces, places(at, t_ref, kv_ref, pieces), sems)

    def sums(step, local, query):
        p = t_ref[at.order + t_ref[at.first] + local]
        attend(t_ref, at.all_list, p, query, kv_ref, acc_ref, m_ref)

    each_span(
        at, offset, count, t_ref, q_ref, pieces, o_refs, acc_ref, worst_ref, run_ref, span_ref, sems.at[0], sums
    )


def attention(q, near, far, near_bases, far_bases, far_first, first_span, span_order, sequence):
    q_spans = q.shape[0] // SPAN
    spans = span_order.shape[0]
    at = Table(spans)
    numbers = jnp.arange(spans, dtype=jnp.int32)
    if far:
        is_far = jnp.logical_and(numbers >= far_first, numbers < far_first + far[0].shape[0])
    else:
        is_far = numbers < 0
    head = jnp.stack([first_span, far_first, *near_bases, *far_bases]).astype(jnp.int32)
    head = jnp.pad(head, (0, at.order - head.shape[0]))
    near_lists = listing(span_order, jnp.logical_not(is_far))
    far_lists = listing(span_order, is_far)
    all_list = listing(span_order, numbers >= 0)[1]
    table = jnp.concatenate([head, span_order, *near_lists, *far_lists, all_list, sequence])
    elements = q.shape[0] * GROUP * spans * SPAN // 2
    n_kv = len(near) + len(far)
    smem, vmem, anywhere = (pl.BlockSpec(memory_space=space) for space in (pltpu.SMEM, pltpu.VMEM, pl.ANY))
    acc_like = pltpu.VMEM((HD + EXTRA, ROWS), jnp.float32)
    m_like = pltpu.VMEM((8, ROWS), jnp.float32)
    kv_like = pltpu.VMEM((spans, SPAN + HD, SPAN), jnp.bfloat16)
    span_like = pltpu.VMEM((SPAN + HD, SPAN), jnp.bfloat16)

    def call(kernel, name, operands, pieces, out_shape, scratch_shapes, part, in_place):
        spaces = [anywhere] * (len(pieces) - in_place) + [vmem] * in_place
        return pl.pallas_call(
            kernel,
            in_specs=[smem] + [vmem] * (len(operands) - 1) + spaces,
            out_specs=[vmem] * len(out_shape),
            out_shape=out_shape,
            scratch_shapes=[*scratch_shapes, pltpu.SemaphoreType.DMA((n_kv,))],
            compiler_params=pltpu.CompilerParams(vmem_limit_bytes=VMEM),
            cost_estimate=pl.CostEstimate(
                flops=int(8 * HD * elements * part),
                bytes_accessed=int(4 * q.size * part) + 4 * spans * SPAN * HD,
                transcendentals=int(elements * part),
            ),
            name=name,
        )(*operands, *pieces)

    def begin(offset, count, q):
        shapes = [
            jax.ShapeDtypeStruct((count, HD + EXTRA, ROWS), jnp.float32),
            jax.ShapeDtypeStruct((count, 8, ROWS), jnp.float32),
        ]
        kernel = functools.partial(near_kernel, at, offset, len(near))
        return call(kernel, "near", (table, q), near, shapes, [kv_like], 0.75 * count / q_spans, len(near))

    def finish(begun, begun_at, offset, count):
        shapes = [jax.ShapeDtypeStruct((SPAN, GROUP * HD), q.dtype)] * count
        kernel = functools.partial(far_kernel, at, offset, offset - begun_at, n_kv, count)
        scratch = [acc_like, m_like, m_like, span_like]
        return call(kernel, "far", (table, q, *begun), near + far, shapes, scratch, 0.25 * count / q_spans, 1)

    def whole(offset, count, q, apart):
        if apart:
            shapes = [jax.ShapeDtypeStruct((SPAN, GROUP * HD), q.dtype)] * count
        else:
            shapes = [jax.ShapeDtypeStruct(q.shape, q.dtype)]
        kernel = functools.partial(whole_kernel, at, offset, n_kv, count)
        scratch = [m_like, kv_like, acc_like, m_like, m_like, span_like]
        return call(kernel, "whole", (table, q), near + far, shapes, scratch, count / q_spans, n_kv)

    return begin, finish, whole


def unpack_kernel(me_ref, *refs):
    parts, (o_ref, sems) = refs[:-2], refs[-2:]
    copies = []
    for index, part in enumerate(parts):
        column = pl.multiple_of((me_ref[0] ^ index) * GROUP * HD, GROUP * HD)
        copies.append(pltpu.make_async_copy(part, o_ref.at[:, pl.ds(column, GROUP * HD)], sems.at[index]))
    for copy in copies:
        copy.start()
    for copy in copies:
        copy.wait()


def to_token_owners(q, begin, finish, whole, me):
    parts = [None] * KVH

    def send(steps, finished):
        for step, done in zip(steps, finished):
            if step:
                done = lax.ppermute(done, GROUP_AXES, [(i, i ^ step) for i in range(KVH)])
            parts[step] = done

    begun = begin(0, sum(map(len, AWAY)), q)
    offset = 0
    for steps in AWAY:
        finished = finish(begun, 0, offset, len(steps))
        send(steps, finished)
        offset += len(steps)
    q, _ = lax.optimization_barrier((q, (finished, [parts[step] for step in AWAY[0]])))
    send(HOME, whole(offset, len(HOME), q, True))
    return pl.pallas_call(
        unpack_kernel,
        in_specs=[pl.BlockSpec(memory_space=pltpu.SMEM)] + [pl.BlockSpec(memory_space=pltpu.VMEM)] * KVH,
        out_specs=pl.BlockSpec(memory_space=pl.ANY),
        out_shape=jax.ShapeDtypeStruct((SPAN, HQ * HD), parts[0].dtype),
        scratch_shapes=[pltpu.SemaphoreType.DMA((KVH,))],
        compiler_params=pltpu.CompilerParams(vmem_limit_bytes=VMEM),
        name="unpack",
    )(me.reshape(1), *parts)


def pack_kernel(k_ref, v_ref, o_ref):
    for h in range(KVH):
        o_ref[h, :SPAN] = k_ref[:, h * HD : (h + 1) * HD]
        o_ref[h, SPAN:] = v_ref[:, h * HD : (h + 1) * HD].T


def to_head_owners(key_rows, value_rows):
    rows = key_rows.shape[0]
    exchange = functools.partial(
        lax.all_to_all, axis_name=GROUP_AXES, split_axis=0, concat_axis=0, tiled=False
    )
    if rows == SPAN:
        packed = pl.pallas_call(
            pack_kernel, out_shape=jax.ShapeDtypeStruct((KVH, SPAN + HD, SPAN), key_rows.dtype), name="pack"
        )(key_rows, value_rows)
        return exchange(packed)
    packed = jnp.concatenate([key_rows.reshape(rows, KVH, HD), value_rows.reshape(rows, KVH, HD)], 2)
    own = exchange(packed.transpose(1, 0, 2)).reshape(KVH * rows // SPAN, SPAN, 2 * HD)
    return jnp.concatenate([own[:, :, :HD], own[:, :, HD:].transpose(0, 2, 1)], 1)


def shards(outer, queries, key_rows, value_rows, span_order):
    rows = queries.shape[0]
    place = lax.axis_index("outer")
    group_rows = KVH * rows
    group_spans = group_rows // SPAN
    own = to_head_owners(key_rows, value_rows)
    q = queries.reshape(rows, KVH, GROUP * HD).transpose(1, 0, 2)
    q = lax.all_to_all(q, GROUP_AXES, split_axis=0, concat_axis=0, tiled=False).reshape(group_rows, GROUP * HD)
    if outer == 4:
        up = lax.ppermute(own, "outer", [(i, (i + 1) % outer) for i in range(outer)])
        down = lax.ppermute(own, "outer", [(i, (i - 1) % outer) for i in range(outer)])
        far = [lax.ppermute(up, "outer", [(i, (i + 1) % outer) for i in range(outer)])]
        near = [own, up, down]
        near_bases = [(place + step) % outer * group_spans for step in (0, outer - 1, 1)]
        far_first = (place + outer - 2) % outer * group_spans
        far_bases = [far_first]
    else:
        near = [lax.all_gather(own, "outer", axis=0, tiled=True)]
        near_bases = [jnp.int32(0)]
        far, far_bases, far_first = [], [], jnp.int32(0)
    me = lax.axis_index(GROUP_AXES).astype(jnp.int32)
    apart = rows == SPAN and outer == 4
    if apart:
        sequence = jnp.stack([me ^ step for steps in (*AWAY, HOME) for step in steps])
    else:
        sequence = jnp.arange(group_spans, dtype=jnp.int32)
    first_span = place * group_spans
    steps = attention(q, near, far, near_bases, far_bases, far_first, first_span, span_order, sequence)
    if apart:
        return to_token_owners(q, *steps, me)
    out = steps[-1](0, group_spans, q, False)[0]
    out = lax.all_to_all(out.reshape(KVH, rows, GROUP * HD), GROUP_AXES, split_axis=0, concat_axis=0, tiled=False)
    return out.transpose(1, 0, 2).reshape(rows, HQ * HD)


def solution(mesh):
    ctx, head = mesh.devices.shape
    inner = KVH // head
    split = Mesh(mesh.devices.reshape(ctx // inner, inner, head), ("outer", "inner", "head"))
    spec = P(("outer", "inner", "head"), None)
    return jax.shard_map(
        functools.partial(shards, ctx // inner),
        mesh=split,
        in_specs=(spec, spec, spec, P()),
        out_specs=spec,
        check_vma=False,
    )
```
